256 devices in a mesh: section: 16 (over y, z_hi), tensor: 16 (over z_lo, x, core).
Axes of the slice: x: 4, y: 4, z: 8 (z_hi: 4, z_lo: 2; z = z_hi * 2 + z_lo), core: 2. Of those that a mesh axis runs over, the one named last changes fastest.
Arguments:
- entering_streams: bfloat16 [16, 4, 128, 5120], P('section', None, 'tensor'), may hold values from -6 to 6
- entering_grads: bfloat16 [16, 4, 128, 5120], P('section', None, 'tensor'), may hold values from -6 to 6
- fresh_streams: bfloat16 [1, 4, 128, 5120], P(None, None, 'tensor'), may hold values from -6 to 6
- loss_grads: bfloat16 [1, 4, 128, 5120], P(None, None, 'tensor'), may hold values from -6 to 6
- stashed: bfloat16 [2, 16, 4, 128, 5120], P(None, 'section', None, 'tensor'), may hold values from -6 to 6
- slot_order: int32 [16, 2], replicated, may hold values from 0 to 1, each once within a row
- q_weight: bfloat16 [16, 5120, 6144], P('section', None, 'tensor'), may hold values from -0.078125 to 0.078125
- kv_weight: bfloat16 [16, 2, 5120, 1024], P('section', None, None, 'tensor'), may hold values from -0.078125 to 0.078125
- out_weight: bfloat16 [16, 6144, 5120], P('section', 'tensor'), may hold values from -0.15625 to 0.15625
- norm_gain: float32 [16, 5120], P('section'), may hold values from 0.1 to 1.9
- head_gains: float32 [16, 2, 128], P('section'), may hold values from 0.6 to 1.8
- stream_in: float32 [16, 4], P('section'), may hold values from 0.1 to 0.6
- stream_out: float32 [16, 4], P('section'), may hold values from 0.5 to 1.5
- stream_mix: float32 [16, 4, 4], P('section'), may hold values from -0.2 to 0.6
Outputs:
- leaving_streams: bfloat16 [16, 4, 128, 5120], P('section', None, 'tensor')
- leaving_grads: bfloat16 [16, 4, 128, 5120], P('section', None, 'tensor')
- evicted: bfloat16 [2, 16, 4, 128, 5120], P(None, 'section', None, 'tensor')
The draws below stay inside these ranges and needn't reach their ends.
Inputs may be any that keep to these rules, and one draw needn't show every extreme that they name: Each row of slot_order is a permutation of 0 to 1.
All inputs are finite; a program needn't handle non-finite values.
Results may differ from the reference program's by a relative error of at most 0.04.
Values may be sent and summed in bfloat16 or wider, within the bound.
No kernel may reach another device: no remote copies, remote signals or barrier semaphores. Data moves between devices by JAX's collectives and lax.ppermute only.
A program may use at most 128 MiB of HBM per device.

```python
import math
import jax
import jax.numpy as jnp
from jax import lax

D = 5120
HD = 128
HQ_DEV = 3
STREAMS = 4
ROWS = 128
TICKS = 2
HQ = 48
KV = 8
N_SECTION = 16
N_TENSOR = 16


def shard_levels(stream_key, extent, cuts, least, largest):
    level, own = 1.0, jax.random.fold_in(stream_key, 6)
    for dim, shards_of in cuts:
        draws = jnp.exp(jax.random.uniform(jax.random.fold_in(own, dim), (shards_of,), jnp.float32, least / len(cuts), largest / len(cuts)))
        level = level * jnp.repeat(draws, extent[dim] // shards_of).reshape([-1 if axis == dim else 1 for axis in range(len(extent))])
    return level


def centred(stream_key, extent, scale, most, split=(), kind=jnp.bfloat16):
    level = shard_levels(stream_key, extent, split, -0.22, 0.18) if split else 1.0
    result = jax.random.normal(stream_key, extent, jnp.float32) * scale * level
    return jnp.minimum(jnp.maximum(result, -most), most).astype(kind)


def setup_inputs(seed: int = 0) -> dict:
    key_of = jax.random.split(jax.random.key(seed), 15)
    return {
        "entering_streams": centred(key_of[0], (N_SECTION, STREAMS, ROWS, D), 1.0, 6.0, ((0, 16), (2, 16))),
        "entering_grads": centred(key_of[1], (N_SECTION, STREAMS, ROWS, D), 1.0, 6.0, ((0, 16), (2, 16))),
        "fresh_streams": centred(key_of[2], (TICKS - 1, STREAMS, ROWS, D), 1.0, 6.0, ((2, 16),)),
        "loss_grads": centred(key_of[3], (TICKS - 1, STREAMS, ROWS, D), 1.0, 6.0, ((2, 16),)),
        "stashed": centred(key_of[4], (TICKS, N_SECTION, STREAMS, ROWS, D), 1.0, 6.0, ((1, 16), (3, 16))),
        "slot_order": jax.vmap(lambda own: jax.random.permutation(own, TICKS))(jax.random.split(key_of[5], N_SECTION)).reshape((N_SECTION, TICKS)).astype(jnp.int32),
        "q_weight": centred(key_of[6], (N_SECTION, D, HQ * HD), D ** -0.5, 0.078125, ((0, 16), (2, 16))),
        "kv_weight": centred(key_of[7], (N_SECTION, 2, D, KV * HD), D ** -0.5, 0.078125, ((0, 16), (3, 16))),
        "out_weight": centred(key_of[8], (N_SECTION, HQ * HD, D), (HQ * HD // 4) ** -0.5, 0.15625, ((0, 16), (1, 16))),
        "norm_gain": jnp.clip(1.0 + 0.18 * jax.random.normal(key_of[9], (N_SECTION, D), jnp.float32), 0.1, 1.9),
        "head_gains": jnp.clip(jnp.exp(math.log(1.8) - 1.0986122 * jax.random.uniform(key_of[10], (N_SECTION, 2, HD), jnp.float32) ** shard_levels(key_of[10], (N_SECTION, 2, HD), ((0, 16),), -0.2, 0.2)), 0.6, 1.8),
        "stream_in": jnp.clip(0.1 + 0.5 * jax.random.uniform(key_of[11], (N_SECTION, STREAMS), jnp.float32) ** shard_levels(key_of[11], (N_SECTION, STREAMS), ((0, 16),), -0.2, 0.2), 0.1, 0.6),
        "stream_out": jnp.clip(0.5 + 1.0 * jax.random.uniform(key_of[12], (N_SECTION, STREAMS), jnp.float32) ** shard_levels(key_of[12], (N_SECTION, STREAMS), ((0, 16),), -0.2, 0.2), 0.5, 1.5),
        "stream_mix": jnp.clip(-0.2 + 0.8 * jax.random.uniform(key_of[13], (N_SECTION, STREAMS, STREAMS), jnp.float32) ** shard_levels(key_of[13], (N_SECTION, STREAMS, STREAMS), ((0, 16),), -0.2, 0.2), -0.2, 0.6),
    }


EPSILON = 1e-06
ROPE_BASE = 1000000.0

def rope_tables(row_count, head_width):
    half_width = head_width // 2
    position = jnp.arange(row_count, dtype=jnp.float32)[:, None]
    frequency = ROPE_BASE ** (-jnp.arange(half_width, dtype=jnp.float32) / half_width)
    angles = position * frequency[None, :]
    return (jnp.cos(angles), jnp.sin(angles))

def rotate_half(values, cosine, sine_table):
    half_width = values.shape[-1] // 2
    first_half = values[..., :half_width]
    second_half = values[..., half_width:]
    cos_rows = cosine[:, None, :]
    sin_rows = sine_table[:, None, :]
    return jnp.concatenate([first_half * cos_rows - second_half * sin_rows, second_half * cos_rows + first_half * sin_rows], axis=-1)

def head_norm(values, scaling):
    return values * lax.rsqrt(lax.optimization_barrier(jnp.mean(values * values, axis=-1, keepdims=True)) + EPSILON) * scaling

def attend_group(queries, key_rows, value_rows, head_gains):
    row_count = queries.shape[0]
    head_width = key_rows.shape[1]
    head_count = queries.shape[1] // head_width
    cosine, sine_table = rope_tables(row_count, head_width)
    query_heads = rotate_half(head_norm(queries.reshape(row_count, head_count, head_width), head_gains[0]), cosine, sine_table)
    key_heads = rotate_half(head_norm(key_rows.reshape(row_count, 1, head_width), head_gains[1]), cosine, sine_table)[:, 0]
    scores = jnp.einsum('qhc,kc->hqk', query_heads, key_heads) / math.sqrt(head_width)
    causal = jnp.arange(row_count)[:, None] >= jnp.arange(row_count)[None, :]
    scores = jnp.where(causal[None], scores, -1e+30)
    scores = scores - lax.stop_gradient(lax.optimization_barrier(jnp.max(scores, axis=-1, keepdims=True)))
    exp_scores = jnp.exp(scores)
    probability = exp_scores / lax.optimization_barrier(jnp.sum(exp_scores, axis=-1, keepdims=True))
    rounded = lax.optimization_barrier(probability.astype(jnp.bfloat16)).astype(jnp.float32)
    context = jnp.einsum('hqk,kc->qhc', rounded, value_rows)
    return context.reshape(row_count, head_count * head_width)

def mixed_input(streams_now, stream_in, norm_gain):
    combined = lax.optimization_barrier(jnp.sum(stream_in[:, None, None] * streams_now, axis=0))
    return combined * lax.rsqrt(lax.optimization_barrier(jnp.mean(combined * combined, axis=-1, keepdims=True)) + EPSILON) * norm_gain

def project(normed, q_weight, kv_weight):
    queries = jnp.dot(normed, q_weight, preferred_element_type=jnp.float32).astype(jnp.bfloat16)
    key_rows = jnp.dot(normed, kv_weight[0], preferred_element_type=jnp.float32).astype(jnp.bfloat16)
    value_rows = jnp.dot(normed, kv_weight[1], preferred_element_type=jnp.float32).astype(jnp.bfloat16)
    return (queries, key_rows, value_rows)

def grouped(queries, key_rows, value_rows):
    query_groups = queries.reshape(ROWS, N_TENSOR, HQ_DEV * HD).transpose(1, 0, 2).astype(jnp.float32)
    key_groups = jnp.repeat(key_rows.reshape(ROWS, KV, HD).transpose(1, 0, 2), 2, axis=0).astype(jnp.float32)
    value_groups = jnp.repeat(value_rows.reshape(ROWS, KV, HD).transpose(1, 0, 2), 2, axis=0).astype(jnp.float32)
    return (query_groups, key_groups, value_groups)

def attend_all(query_groups, key_groups, value_groups, head_gains):
    return jax.vmap(attend_group, in_axes=(0, 0, 0, None))(query_groups, key_groups, value_groups, head_gains)

def layer_forward(streams, params):
    stream_in, stream_out, stream_mix, norm_gain, head_gains, q_weight, kv_weight, out_weight = params
    streams_f = streams.astype(jnp.float32)
    normed = mixed_input(streams_f, stream_in, norm_gain).astype(jnp.bfloat16)
    query_groups, key_groups, value_groups = grouped(*project(normed, q_weight, kv_weight))
    context = attend_all(query_groups, key_groups, value_groups, head_gains).astype(jnp.bfloat16)
    out_groups = out_weight.reshape(N_TENSOR, HQ_DEV * HD, D).astype(jnp.float32)
    partials = jnp.einsum('grc,gcd->grd', context.astype(jnp.float32), out_groups, precision=lax.Precision.HIGHEST)
    partials = lax.optimization_barrier(partials.astype(jnp.bfloat16)).astype(jnp.float32)
    output_rows = lax.optimization_barrier(jnp.sum(partials, axis=0))
    mixed = jnp.tensordot(stream_mix, streams_f, axes=1, precision=lax.Precision.HIGHEST) + stream_out[:, None, None] * output_rows[None]
    return mixed.astype(jnp.bfloat16)

def layer_backward(saved, grads, params):
    stream_in, stream_out, stream_mix, norm_gain, head_gains, q_weight, kv_weight, out_weight = params
    streams_f = saved.astype(jnp.float32)
    grads_f = grads.astype(jnp.float32)

    def pre_layer(streams_now):
        return mixed_input(streams_now, stream_in, norm_gain)
    normed_f, pre_back = jax.vjp(pre_layer, streams_f)
    query_groups, key_groups, value_groups = grouped(*project(normed_f.astype(jnp.bfloat16), q_weight, kv_weight))
    out_grad = jnp.tensordot(stream_out, grads_f, axes=1, precision=lax.Precision.HIGHEST).astype(jnp.bfloat16)
    context_grad = jnp.dot(out_grad, out_weight.T, preferred_element_type=jnp.float32)
    context_groups = context_grad.reshape(ROWS, N_TENSOR, HQ_DEV * HD).transpose(1, 0, 2)

    def attend_inputs(query_in, key_in, value_in):
        return attend_all(query_in, key_in, value_in, head_gains)
    _, attend_back = jax.vjp(attend_inputs, query_groups, key_groups, value_groups)
    query_grad, key_grad, value_grad = attend_back(context_groups)
    query_grad = query_grad.astype(jnp.bfloat16).transpose(1, 0, 2).reshape(ROWS, HQ * HD)
    key_grad = lax.optimization_barrier(key_grad.astype(jnp.bfloat16)).astype(jnp.float32).reshape(KV, 2, ROWS, HD)
    value_grad = lax.optimization_barrier(value_grad.astype(jnp.bfloat16)).astype(jnp.float32).reshape(KV, 2, ROWS, HD)
    key_w = kv_weight[0].astype(jnp.float32).reshape(D, KV, HD)
    value_w = kv_weight[1].astype(jnp.float32).reshape(D, KV, HD)
    normed_grad = jnp.dot(query_grad, q_weight.T, preferred_element_type=jnp.float32)
    normed_grad = normed_grad + jnp.einsum('hprc,dhc->rd', key_grad, key_w, precision=lax.Precision.HIGHEST)
    normed_grad = normed_grad + jnp.einsum('hprc,dhc->rd', value_grad, value_w, precision=lax.Precision.HIGHEST)
    streams_grad = jnp.tensordot(stream_mix.T, grads_f, axes=1, precision=lax.Precision.HIGHEST) + pre_back(normed_grad)[0]
    return streams_grad.astype(jnp.bfloat16)

def reference(entering_streams, entering_grads, fresh_streams, loss_grads, stashed, slot_order, q_weight, kv_weight, out_weight, norm_gain, head_gains, stream_in, stream_out, stream_mix):
    half_sections = N_SECTION // 2
    forward_now = entering_streams
    backward_now = entering_grads
    evicted_list = []
    forward_out = entering_streams
    backward_out = entering_grads
    for step_index in range(TICKS):
        forward_list = []
        backward_list = []
        for section_index in range(N_SECTION):
            params = (stream_in[section_index], stream_out[section_index], stream_mix[section_index], norm_gain[section_index], head_gains[section_index], q_weight[section_index], kv_weight[section_index], out_weight[section_index])
            partner = (section_index + half_sections) % N_SECTION
            slot = slot_order[section_index, step_index].astype(jnp.int32)
            saved = lax.dynamic_index_in_dim(stashed, slot, 0, keepdims=False)[partner]
            forward_list.append(layer_forward(forward_now[section_index], params))
            backward_list.append(layer_backward(saved, backward_now[section_index], params))
        evicted_list.append(jnp.stack([forward_now[(section_index + half_sections) % N_SECTION] for section_index in range(N_SECTION)]))
        forward_out = jnp.stack(forward_list)
        backward_out = jnp.stack(backward_list)
        if step_index + 1 < TICKS:
            forward_now = jnp.concatenate([fresh_streams[step_index][None], forward_out[:-1]], axis=0)
            backward_now = jnp.concatenate([backward_out[1:], loss_grads[step_index][None]], axis=0)
    return (forward_out, backward_out, jnp.stack(evicted_list))
```

```python
import math

import jax
import jax.numpy as jnp
import numpy as np
from jax import lax
from jax.experimental import pallas as pl
from jax.experimental.pallas import tpu as pltpu
from jax.sharding import PartitionSpec as P

EPSILON = 1e-06
ROPE_BASE = 1000000.0
ROWS = 128
LOCAL = 8
HEAD = 128
WIDTH = 5120
CHUNK = 1280
STEPS = WIDTH // CHUNK
QUERY = 384
BOTH = 256
GROUPS = [[core + 2 * chip for chip in range(8)] for core in range(2)]


def other_core(value):
    return lax.ppermute(value, "tensor", [(i, i ^ 1) for i in range(16)])


def to_partner(value):
    return lax.ppermute(value, "section", [(i, i ^ 8) for i in range(16)])


def shifted(value, by):
    return lax.ppermute(value, "section", [(i, (i + by) % 16) for i in range(16)])


def token_order(parity):
    own = [2 * chip + parity for chip in range(8)]
    other = [2 * chip + 1 - parity for chip in range(8)]
    return np.concatenate([np.arange(LOCAL) + LOCAL * block for block in own + other])


def rope_of(order):
    half = HEAD // 2
    position = jnp.asarray(order, jnp.float32)[:, None]
    frequency = ROPE_BASE ** (-jnp.arange(half, dtype=jnp.float32) / half)
    angles = position * frequency[None, :]
    return jnp.stack([jnp.cos(angles), jnp.sin(angles)])


def dot(left, right):
    return jnp.dot(left, right, preferred_element_type=jnp.float32)


def dot_nt(left, right):
    return lax.dot_general(left, right, (((1,), (1,)), ((), ())), preferred_element_type=jnp.float32)


def dot_tn(left, right):
    return lax.dot_general(left, right, (((0,), (0,)), ((), ())), preferred_element_type=jnp.float32)


def rope(values, cosine, sine):
    return values * cosine + pltpu.roll(values, HEAD // 2, 1) * sine


def rope_back(grads, cosine, sine):
    return grads * cosine - pltpu.roll(grads, HEAD // 2, 1) * sine


def norm_scale(values):
    return lax.rsqrt(jnp.mean(values * values, axis=-1, keepdims=True) + EPSILON)


def head_back(grads, values, scale, gain):
    weighted = grads * gain
    inner = jnp.mean(values * weighted, axis=-1, keepdims=True)
    return scale * weighted - values * (scale * scale * scale * inner)


def softmax_of(query_head, key_head, mask):
    scores = dot_nt(query_head, key_head) * (1.0 / math.sqrt(HEAD)) + mask
    scores = scores - jnp.max(scores, axis=-1, keepdims=True)
    weights = jnp.exp(scores)
    return weights / jnp.sum(weights, axis=-1, keepdims=True)


def attend(projected, gains, cosine, sine, mask):
    bf16, f32 = jnp.bfloat16, jnp.float32
    keys = projected[:, QUERY : QUERY + HEAD].astype(f32)
    key_head = rope(keys * norm_scale(keys) * gains[1:2], cosine, sine).astype(bf16)
    values = projected[:, QUERY + HEAD :]
    context = []
    for head in range(QUERY // HEAD):
        queries = projected[:, head * HEAD : (head + 1) * HEAD].astype(f32)
        query_head = rope(queries * norm_scale(queries) * gains[0:1], cosine, sine).astype(bf16)
        weights = softmax_of(query_head, key_head, mask)
        context.append(dot(weights.astype(bf16), values).astype(bf16))
    return jnp.concatenate(context, axis=1)


def attend_back(projected, context_grad, gains, cosine, sine, mask):
    bf16, f32 = jnp.bfloat16, jnp.float32
    root = 1.0 / math.sqrt(HEAD)
    keys = projected[:, QUERY : QUERY + HEAD].astype(f32)
    key_scale = norm_scale(keys)
    key_head = rope(keys * key_scale * gains[1:2], cosine, sine).astype(bf16)
    values = projected[:, QUERY + HEAD :]
    query_grads = []
    key_total = jnp.zeros((ROWS, HEAD), f32)
    value_total = jnp.zeros((ROWS, HEAD), f32)
    for head in range(QUERY // HEAD):
        queries = projected[:, head * HEAD : (head + 1) * HEAD].astype(f32)
        query_scale = norm_scale(queries)
        query_head = rope(queries * query_scale * gains[0:1], cosine, sine).astype(bf16)
        weights = softmax_of(query_head, key_head, mask)
        upstream = context_grad[:, head * HEAD : (head + 1) * HEAD].astype(bf16)
        value_total = value_total + dot_tn(weights.astype(bf16), upstream)
        weights_grad = dot_nt(upstream, values).astype(bf16).astype(f32)
        inner = jnp.sum(weights * weights_grad, axis=-1, keepdims=True)
        scores_grad = (weights * (weights_grad - inner) * root).astype(bf16)
        key_total = key_total + dot_tn(scores_grad, query_head)
        turned = rope_back(dot(scores_grad, key_head), cosine, sine)
        query_grads.append(head_back(turned, queries, query_scale, gains[0:1]).astype(bf16))
    key_grad = head_back(rope_back(key_total, cosine, sine), keys, key_scale, gains[1:2])
    both = jnp.concatenate([key_grad.astype(bf16), value_total.astype(bf16)], axis=1)
    return jnp.concatenate(query_grads, axis=1), both


def forward_kernel(
    own, other, queries_w, keys_values_w, output_w, gains, cosine, sine, mask, out, total, context
):
    step = pl.program_id(0)

    @pl.when(step == 0)
    def _():
        total[...] = jnp.zeros_like(total)

    @pl.when(step < STEPS)
    def _():
        rows = jnp.concatenate([own[...], other[...]], axis=0)
        total[:, :QUERY] += dot(rows, queries_w[...])
        total[:, QUERY:] += dot_nt(rows, keys_values_w[...])

    @pl.when(step == STEPS - 1)
    def _():
        projected = total[...].astype(jnp.bfloat16)
        context[...] = attend(projected, gains[...], cosine[...], sine[...], mask[...])

    @pl.when(step >= STEPS)
    def _():
        out[...] = dot(context[...], output_w[...]).astype(out.dtype)


def project_kernel(rows, queries_w, keys_values_w, turn, out, total):
    step = pl.program_id(0)

    @pl.when(step == 0)
    def _():
        total[...] = jnp.zeros_like(total)

    total[:, :QUERY] += dot(rows[...], queries_w[...])
    total[:, QUERY:] += dot_nt(rows[...], keys_values_w[...])

    @pl.when(step == STEPS - 1)
    def _():
        out[...] = dot(turn[...], total[...].astype(jnp.bfloat16)).astype(out.dtype)


def backward_kernel(
    own, other, projected, queries_w, keys_values_w, output_w, gains, cosine, sine, mask, out, total, query_grad, both_grad
):
    step = pl.program_id(0)

    @pl.when(step == 0)
    def _():
        total[...] = jnp.zeros_like(total)

    @pl.when(step < STEPS)
    def _():
        rows = jnp.concatenate([own[...], other[...]], axis=0)
        total[...] += dot_nt(rows, output_w[...])

    @pl.when(step == STEPS - 1)
    def _():
        query_part, both_part = attend_back(
            projected[...], total[...], gains[...], cosine[...], sine[...], mask[...]
        )
        query_grad[...] = query_part
        both_grad[...] = both_part

    @pl.when(step >= STEPS)
    def _():
        part = dot_nt(query_grad[...], queries_w[...]) + dot(both_grad[...], keys_values_w[...])
        out[...] = part.astype(out.dtype)


def first_phase(step):
    return jnp.minimum(step, STEPS - 1)


def second_phase(step):
    return jnp.maximum(step - STEPS, 0)


def whole(shape):
    return pl.BlockSpec(shape, lambda step: (0,) * len(shape))


PARAMS = pltpu.CompilerParams(vmem_limit_bytes=40 * 2**20)
SMALL = [whole((2, HEAD)), whole((ROWS, HEAD)), whole((ROWS, HEAD)), whole((ROWS, ROWS))]


def run_forward(own, other, weights, small):
    return pl.pallas_call(
        forward_kernel,
        grid=(2 * STEPS,),
        out_shape=jax.ShapeDtypeStruct((ROWS, WIDTH), jnp.bfloat16),
        in_specs=[
            pl.BlockSpec((ROWS // 2, CHUNK), lambda step: (0, first_phase(step))),
            pl.BlockSpec((ROWS // 2, CHUNK), lambda step: (0, first_phase(step))),
            pl.BlockSpec((CHUNK, QUERY), lambda step: (first_phase(step), 0)),
            pl.BlockSpec((BOTH, CHUNK), lambda step: (0, first_phase(step))),
            pl.BlockSpec((QUERY, CHUNK), lambda step: (0, second_phase(step))),
        ]
        + SMALL,
        out_specs=pl.BlockSpec((ROWS, CHUNK), lambda step: (0, second_phase(step))),
        scratch_shapes=[
            pltpu.VMEM((ROWS, QUERY + BOTH), jnp.float32),
            pltpu.VMEM((ROWS, QUERY), jnp.bfloat16),
        ],
        compiler_params=PARAMS,
        cost_estimate=pl.CostEstimate(flops=1500000000, bytes_accessed=14000000, transcendentals=50000),
    )(own, other, *weights, *small)


def run_project(rows, weights, turn):
    return pl.pallas_call(
        project_kernel,
        grid=(STEPS,),
        out_shape=jax.ShapeDtypeStruct((ROWS, QUERY + BOTH), jnp.bfloat16),
        in_specs=[
            pl.BlockSpec((ROWS, CHUNK), lambda step: (0, step)),
            pl.BlockSpec((CHUNK, QUERY), lambda step: (step, 0)),
            pl.BlockSpec((BOTH, CHUNK), lambda step: (0, step)),
            whole((ROWS, ROWS)),
        ],
        out_specs=whole((ROWS, QUERY + BOTH)),
        scratch_shapes=[pltpu.VMEM((ROWS, QUERY + BOTH), jnp.float32)],
        compiler_params=PARAMS,
        cost_estimate=pl.CostEstimate(flops=900000000, bytes_accessed=8000000, transcendentals=0),
    )(rows, weights[0], weights[1], turn)


def run_backward(own, other, projected, weights, small):
    return pl.pallas_call(
        backward_kernel,
        grid=(2 * STEPS,),
        out_shape=jax.ShapeDtypeStruct((ROWS, WIDTH), jnp.bfloat16),
        in_specs=[
            pl.BlockSpec((ROWS // 2, CHUNK), lambda step: (0, first_phase(step))),
            pl.BlockSpec((ROWS // 2, CHUNK), lambda step: (0, first_phase(step))),
            whole((ROWS, QUERY + BOTH)),
            pl.BlockSpec((CHUNK, QUERY), lambda step: (second_phase(step), 0)),
            pl.BlockSpec((BOTH, CHUNK), lambda step: (0, second_phase(step))),
            pl.BlockSpec((QUERY, CHUNK), lambda step: (0, first_phase(step))),
        ]
        + SMALL,
        out_specs=pl.BlockSpec((ROWS, CHUNK), lambda step: (0, second_phase(step))),
        scratch_shapes=[
            pltpu.VMEM((ROWS, QUERY), jnp.float32),
            pltpu.VMEM((ROWS, QUERY), jnp.bfloat16),
            pltpu.VMEM((ROWS, BOTH), jnp.bfloat16),
        ],
        compiler_params=PARAMS,
        cost_estimate=pl.CostEstimate(flops=1500000000, bytes_accessed=14000000, transcendentals=50000),
    )(own, other, projected, *weights, *small)


def mixed(weights, offset, stride, streams):
    return sum(weights[offset + i * stride] * streams[i] for i in range(4))


def norm_kernel(mix_in, streams, gain, copies, combined, scale):
    total = mixed(mix_in, 0, 1, streams[...].astype(jnp.float32))
    row_scale = norm_scale(total)
    normed = (total * row_scale * gain[...]).astype(copies.dtype)
    combined[...] = total
    scale[...] = jnp.broadcast_to(row_scale, scale.shape)
    if len(copies.shape) == 2:
        copies[...] = normed
    else:
        for chip in range(8):
            copies[chip] = normed


def grad_kernel(mix_out, grads, copies):
    out_grad = mixed(mix_out, 0, 1, grads[...].astype(jnp.float32)).astype(copies.dtype)
    for chip in range(8):
        copies[chip] = out_grad


def forward_end_kernel(mix_out, mix, landed, streams, out):
    rows = jnp.sum(landed[...].astype(jnp.float32), axis=0)
    streams_f = streams[...].astype(jnp.float32)
    for i in range(4):
        out[i] = (mixed(mix, 4 * i, 1, streams_f) + mix_out[i] * rows).astype(out.dtype)


def backward_end_kernel(mix_in, mix, landed, grads, gain, combined, scale, out):
    weighted = jnp.sum(landed[...].astype(jnp.float32), axis=0) * gain[...]
    row_scale = scale[:, :1]
    inner = jnp.mean(weighted * combined[...], axis=-1, keepdims=True)
    combined_grad = row_scale * weighted - combined[...] * (row_scale * row_scale * row_scale * inner)
    grads_f = grads[...].astype(jnp.float32)
    for j in range(4):
        out[j] = (mixed(mix, j, 4, grads_f) + mix_in[j] * combined_grad).astype(out.dtype)


def plain(kernel, scalars, arrays, outs):
    smem, vmem = pl.BlockSpec(memory_space=pltpu.SMEM), pl.BlockSpec(memory_space=pltpu.VMEM)
    return pl.pallas_call(
        kernel,
        out_shape=[jax.ShapeDtypeStruct(*out) for out in outs],
        in_specs=[smem] * len(scalars) + [vmem] * len(arrays),
        out_specs=[vmem] * len(outs),
        compiler_params=PARAMS,
        cost_estimate=pl.CostEstimate(flops=4000000, bytes_accessed=3000000, transcendentals=0),
    )(*scalars, *arrays)


def gathered(copies):
    own = lax.all_to_all(copies, "tensor", 0, 0, axis_index_groups=GROUPS, tiled=True)
    own = own.reshape(ROWS // 2, -1)
    return own, other_core(own)


def scattered(partial):
    received = other_core(partial[ROWS // 2 :])
    pair = partial[: ROWS // 2].astype(jnp.float32) + received.astype(jnp.float32)
    pair = pair.astype(jnp.bfloat16).reshape(8, LOCAL, -1)
    return lax.all_to_all(pair, "tensor", 0, 0, axis_index_groups=GROUPS, tiled=True)


def on_device(
    entering_streams,
    entering_grads,
    fresh_streams,
    loss_grads,
    stashed,
    slot_order,
    q_weight,
    kv_weight,
    out_weight,
    norm_gain,
    head_gains,
    stream_in,
    stream_out,
    stream_mix,
):
    section = lax.axis_index("section")
    parity = lax.axis_index("tensor") % 2
    partner = (section + 8) % 16
    queries_w, output_w = q_weight[0], out_weight[0]
    gain, gains = norm_gain[0], head_gains[0]
    mix_in, mix_out, mix = stream_in[0], stream_out[0], stream_mix[0]
    bf16, f32 = jnp.bfloat16, jnp.float32

    def chosen(build):
        return jnp.where(parity == 0, build(token_order(0)), build(token_order(1)))

    cosine = chosen(lambda order: jnp.concatenate([rope_of(order)[0]] * 2, axis=1))
    sine = chosen(lambda order: jnp.concatenate([-rope_of(order)[1], rope_of(order)[1]], axis=1))
    mask = chosen(lambda order: jnp.where(order[:, None] >= order[None, :], 0.0, -1e30).astype(f32))
    turn = chosen(lambda order: jnp.asarray(order[:, None] == np.arange(ROWS)[None, :], bf16))

    halves = jnp.swapaxes(kv_weight[0], 1, 2)
    others = other_core(halves)
    keys_values_w = jnp.where(
        parity == 0,
        jnp.concatenate([halves, others], axis=1),
        jnp.concatenate([others, halves], axis=1),
    ).reshape(2 * HEAD, -1)

    weights = (queries_w, keys_values_w, output_w)
    small = (gains, cosine, sine, mask)
    gain_row = gain[None]
    mix_flat = mix.reshape(16)
    row_shape, streams_shape = (LOCAL, WIDTH), (4, LOCAL, WIDTH)

    def normalise(streams, copied):
        first = ((8,) + row_shape if copied else row_shape, bf16)
        outs = [first, (row_shape, f32), ((LOCAL, HEAD), f32)]
        return plain(norm_kernel, [mix_in], [streams, gain_row], outs)

    def out_grad_of(grads):
        return plain(grad_kernel, [mix_out], [grads], [((8,) + row_shape, bf16)])[0]

    def forward_end(streams, landed):
        return plain(forward_end_kernel, [mix_out, mix_flat], [landed, streams], [(streams_shape, bf16)])[0]

    def backward_end(state, grads, landed):
        return plain(
            backward_end_kernel,
            [mix_in, mix_flat],
            [landed, grads, gain_row, *state],
            [(streams_shape, bf16)],
        )[0]

    stash = stashed[:, 0]
    first_slot = slot_order[partner, 0]
    forward_now, backward_now = entering_streams[0], entering_grads[0]
    saved = [
        to_partner(lax.dynamic_index_in_dim(stash, slot, 0, keepdims=False))
        for slot in (first_slot, 1 - first_slot)
    ]
    evicted_first = to_partner(forward_now)

    normed_own, normed_other = gathered(normalise(forward_now, True)[0])
    grad_own, grad_other = gathered(out_grad_of(backward_now))

    states, projected = [], []
    for streams in saved:
        normed, combined, scale = normalise(streams, False)
        states.append((combined, scale))
        rows = lax.all_gather(normed, "tensor", axis=0, tiled=True)
        projected.append(run_project(rows, weights, turn))

    landed = scattered(run_forward(normed_own, normed_other, weights, small))
    forward_out = forward_end(forward_now, landed)
    from_previous = shifted(forward_out, 1)

    landed = scattered(run_backward(grad_own, grad_other, projected[0], weights, small))
    backward_out = backward_end(states[0], backward_now, landed)
    from_following = shifted(backward_out, -1)

    forward_now = jnp.where(section == 0, fresh_streams[0], from_previous)
    evicted_second = to_partner(forward_now)
    normed_own, normed_other = gathered(normalise(forward_now, True)[0])
    landed_forward = scattered(run_forward(normed_own, normed_other, weights, small))

    backward_now = jnp.where(section == 15, loss_grads[0], from_following)
    grad_own, grad_other = gathered(out_grad_of(backward_now))
    landed_backward = scattered(run_backward(grad_own, grad_other, projected[1], weights, small))
    forward_out = forward_end(forward_now, landed_forward)
    backward_out = backward_end(states[1], backward_now, landed_backward)
    evicted = jnp.stack([evicted_first, evicted_second])
    return (forward_out[None], backward_out[None], evicted[:, None])


def solution(mesh):
    return jax.shard_map(
        on_device,
        mesh=mesh,
        in_specs=(
            P("section", None, "tensor", None),
            P("section", None, "tensor", None),
            P(None, None, "tensor", None),
            P(None, None, "tensor", None),
            P(None, "section", None, "tensor", None),
            P(),
            P("section", None, "tensor"),
            P("section", None, None, "tensor"),
            P("section", "tensor", None),
            P("section", None),
            P("section", None, None),
            P("section", None),
            P("section", None),
            P("section", None, None),
        ),
        out_specs=(
            P("section", None, "tensor", None),
            P("section", None, "tensor", None),
            P(None, "section", None, "tensor", None),
        ),
        check_vma=False,
    )
```

```python
import functools
import math

import jax
import jax.numpy as jnp
import numpy as np
from jax import lax
from jax.experimental import pallas as pl
from jax.experimental.pallas import tpu as pltpu
from jax.sharding import PartitionSpec as P

EPSILON = 1e-06
ROPE_BASE = 1000000.0
ROWS = 128
LOCAL = 8
HEAD = 128
WIDTH = 5120
CHUNK = 2560
STEPS = WIDTH // CHUNK
QUERY = 384
BOTH = 256
GROUPS = [[core + 2 * chip for chip in range(8)] for core in range(2)]


def other_core(value):
    return lax.ppermute(value, "tensor", [(i, i ^ 1) for i in range(16)])


def to_partner(value):
    return lax.ppermute(value, "section", [(i, i ^ 8) for i in range(16)])


def shifted(value, by):
    return lax.ppermute(value, "section", [(i, (i + by) % 16) for i in range(16)])


def token_order(parity):
    own = [2 * chip + parity for chip in range(8)]
    other = [2 * chip + 1 - parity for chip in range(8)]
    return np.concatenate([np.arange(LOCAL) + LOCAL * block for block in own + other])


def tables_of(order):
    half = HEAD // 2
    frequency = np.float32(ROPE_BASE) ** (-np.arange(half, dtype=np.float32) / np.float32(half))
    angles = order.astype(np.float32)[:, None] * frequency[None, :]
    cosine, sine = np.cos(angles), np.sin(angles)
    mask = np.where(order[:, None] >= order[None, :], 0.0, -1e30)
    turn = order[:, None] == np.arange(ROWS)[None, :]
    planes = [np.concatenate([cosine, cosine], 1), np.concatenate([-sine, sine], 1), mask, turn]
    return np.stack(planes).astype(np.float32)


TABLES = np.stack([tables_of(token_order(0)), tables_of(token_order(1))])


def dot(left, right):
    return jnp.dot(left, right, preferred_element_type=jnp.float32)


def dot_nt(left, right):
    return lax.dot_general(left, right, (((1,), (1,)), ((), ())), preferred_element_type=jnp.float32)


def dot_tn(left, right):
    return lax.dot_general(left, right, (((0,), (0,)), ((), ())), preferred_element_type=jnp.float32)


def rope(values, cosine, sine):
    return values * cosine + pltpu.roll(values, HEAD // 2, 1) * sine


def rope_back(grads, cosine, sine):
    return grads * cosine - pltpu.roll(grads, HEAD // 2, 1) * sine


def norm_scale(values):
    return lax.rsqrt(jnp.mean(values * values, axis=-1, keepdims=True) + EPSILON)


def head_back(grads, values, scale, gain):
    weighted = grads * gain
    inner = jnp.mean(values * weighted, axis=-1, keepdims=True)
    return scale * weighted - values * (scale * scale * scale * inner)


def softmax_of(query_head, key_head, mask):
    scores = dot_nt(query_head, key_head) * (1.0 / math.sqrt(HEAD)) + mask
    scores = scores - jnp.max(scores, axis=-1, keepdims=True)
    weights = jnp.exp(scores)
    return weights / jnp.sum(weights, axis=-1, keepdims=True)


def joined(own, other, parity):
    first = jnp.where(parity == 0, own, other)
    second = jnp.where(parity == 0, other, own)
    return jnp.concatenate([first, second], axis=1)


def ordered(total, parity):
    own, other = total[:, QUERY : QUERY + HEAD], total[:, QUERY + HEAD :]
    half = HEAD // 2
    keys = joined(own[:, :half], other[:, :half], parity)
    values = joined(own[:, half:], other[:, half:], parity)
    return jnp.concatenate([total[:, :QUERY], keys, values], axis=1).astype(jnp.bfloat16)


def attend(projected, gains, cosine, sine, mask):
    bf16, f32 = jnp.bfloat16, jnp.float32
    keys = projected[:, QUERY : QUERY + HEAD].astype(f32)
    key_head = rope(keys * norm_scale(keys) * gains[1:2], cosine, sine).astype(bf16)
    values = projected[:, QUERY + HEAD :]
    context = []
    for head in range(QUERY // HEAD):
        queries = projected[:, head * HEAD : (head + 1) * HEAD].astype(f32)
        query_head = rope(queries * norm_scale(queries) * gains[0:1], cosine, sine).astype(bf16)
        weights = softmax_of(query_head, key_head, mask)
        context.append(dot(weights.astype(bf16), values).astype(bf16))
    return jnp.concatenate(context, axis=1)


def attend_back(projected, context_grad, gains, cosine, sine, mask, parity):
    bf16, f32 = jnp.bfloat16, jnp.float32
    root = 1.0 / math.sqrt(HEAD)
    keys = projected[:, QUERY : QUERY + HEAD].astype(f32)
    key_scale = norm_scale(keys)
    key_head = rope(keys * key_scale * gains[1:2], cosine, sine).astype(bf16)
    values = projected[:, QUERY + HEAD :]
    query_grads = []
    key_total = jnp.zeros((ROWS, HEAD), f32)
    value_total = jnp.zeros((ROWS, HEAD), f32)
    for head in range(QUERY // HEAD):
        queries = projected[:, head * HEAD : (head + 1) * HEAD].astype(f32)
        query_scale = norm_scale(queries)
        query_head = rope(queries * query_scale * gains[0:1], cosine, sine).astype(bf16)
        weights = softmax_of(query_head, key_head, mask)
        upstream = context_grad[:, head * HEAD : (head + 1) * HEAD].astype(bf16)
        value_total = value_total + dot_tn(weights.astype(bf16), upstream)
        weights_grad = dot_nt(upstream, values).astype(bf16).astype(f32)
        inner = jnp.sum(weights * weights_grad, axis=-1, keepdims=True)
        scores_grad = (weights * (weights_grad - inner) * root).astype(bf16)
        key_total = key_total + dot_tn(scores_grad, query_head)
        turned = rope_back(dot(scores_grad, key_head), cosine, sine)
        query_grads.append(head_back(turned, queries, query_scale, gains[0:1]).astype(bf16))
    key_grad = head_back(rope_back(key_total, cosine, sine), keys, key_scale, gains[1:2])
    half = HEAD // 2
    own = joined(key_grad[:, :half], value_total[:, :half], 0)
    other = joined(key_grad[:, half:], value_total[:, half:], 0)
    first = jnp.where(parity == 0, own, other)
    second = jnp.where(parity == 0, other, own)
    return jnp.concatenate(query_grads, axis=1), first.astype(bf16), second.astype(bf16)


PARAMS = pltpu.CompilerParams(vmem_limit_bytes=62 * 2**20)
SCALAR = pl.BlockSpec(memory_space=pltpu.SMEM)
FAR = pl.BlockSpec(memory_space=pl.ANY)
HALF = ROWS // 2
HALF_ROWS = jax.ShapeDtypeStruct((HALF, WIDTH), jnp.bfloat16)
BF = jnp.bfloat16


def started(copies):
    for copy in copies:
        copy.start()
    return copies


def waited(copies):
    for copy in copies:
        copy.wait()


def columns(chunk):
    return pl.ds(chunk * CHUNK, CHUNK)


def query_loads(queries_w, own_w, other_w, near, sems):
    near_q, near_own, near_other = near
    return [
        [
            pltpu.make_async_copy(
                queries_w.at[columns(c), :], near_q.at[columns(c), :], sems.at[c, 0]
            ),
            pltpu.make_async_copy(own_w.at[:, columns(c)], near_own.at[:, columns(c)], sems.at[c, 1]),
            pltpu.make_async_copy(
                other_w.at[:, columns(c)], near_other.at[:, columns(c)], sems.at[c, 2]
            ),
        ]
        for c in range(STEPS)
    ]


def output_loads(output_w, near, sems):
    return [
        [pltpu.make_async_copy(output_w.at[:, columns(c)], near.at[:, columns(c)], sems.at[c])]
        for c in range(STEPS)
    ]


def row_loads(own, other, rows, sems, part=0):
    if other is None:
        return [pltpu.make_async_copy(own, rows, sems.at[0])]
    source = pl.ds(part * WIDTH, WIDTH)
    return [
        pltpu.make_async_copy(own.at[:, source], rows.at[pl.ds(0, HALF), :], sems.at[0]),
        pltpu.make_async_copy(other.at[:, source], rows.at[pl.ds(HALF, HALF), :], sems.at[1]),
    ]


def stores(near, mine, theirs, c, sems):
    return [
        pltpu.make_async_copy(
            near.at[pl.ds(HALF, HALF), columns(c)], theirs.at[:, columns(c)], sems.at[c, 0]
        ),
        pltpu.make_async_copy(
            near.at[pl.ds(0, HALF), columns(c)], mine.at[:, columns(c)], sems.at[c, 1]
        ),
    ]


def project_chunks(rows, near, loads):
    near_q, near_own, near_other = near
    queries = own = other = 0.0
    for c in range(STEPS):
        waited(loads[c])
        part = rows[:, c * CHUNK : (c + 1) * CHUNK]
        queries += dot(part, near_q[c * CHUNK : (c + 1) * CHUNK, :])
        own += dot_nt(part, near_own[:, c * CHUNK : (c + 1) * CHUNK])
        other += dot_nt(part, near_other[:, c * CHUNK : (c + 1) * CHUNK])
    return jnp.concatenate([queries, own, other], axis=1)


WEIGHT_SCRATCH = [
    pltpu.VMEM((WIDTH, QUERY), BF),
    pltpu.VMEM((HEAD, WIDTH), BF),
    pltpu.VMEM((HEAD, WIDTH), BF),
    pltpu.SemaphoreType.DMA((STEPS, 3)),
]
ROW_SCRATCH = [pltpu.VMEM((ROWS, WIDTH), BF), pltpu.SemaphoreType.DMA((2,))]
SMALL_SCRATCH = [
    pltpu.VMEM((2, HEAD), jnp.float32),
    pltpu.VMEM((4, ROWS, HEAD), jnp.float32),
    pltpu.SemaphoreType.DMA((2,)),
]
OUT_SCRATCH = [pltpu.VMEM((ROWS, WIDTH), BF), pltpu.SemaphoreType.DMA((STEPS, 2))]


def small_loads(gains, tables, near_gains, near_tables, sems):
    return [
        pltpu.make_async_copy(gains, near_gains, sems.at[0]),
        pltpu.make_async_copy(tables, near_tables, sems.at[1]),
    ]


def forward_kernel(
    turned, parity, *refs
):
    own, other = refs[0], None if turned else refs[1]
    queries_w, own_w, other_w, output_w, gains, tables, _, *rest = refs[1 if turned else 2 :]
    mine, theirs, near_q, near_own, near_other, weight_sems, rows, row_sems = rest[:8]
    near_gains, near_tables, small_sems, near_out, out_sems, near_output_w, output_sems = rest[8:15]
    near = (near_q, near_own, near_other)
    row_copies = started(row_loads(own, other, rows, row_sems))
    loads = [started(part) for part in query_loads(queries_w, own_w, other_w, near, weight_sems)]
    small_copies = started(small_loads(gains, tables, near_gains, near_tables, small_sems))
    output_copies = [started(part) for part in output_loads(output_w, near_output_w, output_sems)]
    waited(row_copies)
    projected = ordered(project_chunks(rows, near, loads), parity[0])
    waited(small_copies)
    if turned:
        projected = dot(near_tables[3].astype(BF), projected).astype(BF)
    context = attend(projected, near_gains[...], near_tables[0], near_tables[1], near_tables[2])
    sent = []
    for c in range(STEPS):
        waited(output_copies[c])
        part = dot(context, near_output_w[:, c * CHUNK : (c + 1) * CHUNK])
        near_out[:, c * CHUNK : (c + 1) * CHUNK] = part.astype(BF)
        sent += started(stores(near_out, mine, theirs, c, out_sems))
    waited(sent)


def project_kernel(
    parity, own, queries_w, own_w, other_w, tables, after, out,
    near_q, near_own, near_other, weight_sems, rows, row_sems, near_turn, near_out, sems,
):
    del after
    near = (near_q, near_own, near_other)
    row_copies = started(row_loads(own, None, rows, row_sems))
    loads = [started(part) for part in query_loads(queries_w, own_w, other_w, near, weight_sems)]
    table_copy = started([pltpu.make_async_copy(tables.at[3], near_turn, sems.at[0])])
    waited(row_copies)
    projected = ordered(project_chunks(rows, near, loads), parity[0])
    waited(table_copy)
    near_out[...] = dot(near_turn[...].astype(BF), projected).astype(BF)
    waited(started([pltpu.make_async_copy(near_out, out, sems.at[1])]))


def context_kernel(
    part, own, other, output_w, after, out, rows, row_sems, near_output_w, output_sems, near_out, sems
):
    del after
    row_copies = started(row_loads(own, other, rows, row_sems, part))
    output_copies = [started(chunk) for chunk in output_loads(output_w, near_output_w, output_sems)]
    waited(row_copies)
    near_out[...] = context_chunks(rows, near_output_w, output_copies)
    waited(started([pltpu.make_async_copy(near_out, out, sems.at[0])]))


def context_chunks(rows, near_output_w, output_copies):
    context_grad = 0.0
    for c in range(STEPS):
        waited(output_copies[c])
        part = slice(c * CHUNK, (c + 1) * CHUNK)
        context_grad += dot_nt(rows[:, part], near_output_w[:, part])
    return context_grad


def grads_out(grads, near, loads, near_out, mine, theirs, out_sems):
    query_grad, own_grad, other_grad = grads
    near_q, near_own, near_other = near
    sent = []
    for c in range(STEPS):
        waited(loads[c])
        part = slice(c * CHUNK, (c + 1) * CHUNK)
        total = dot_nt(query_grad, near_q[part, :])
        total = total + dot(own_grad, near_own[:, part]) + dot(other_grad, near_other[:, part])
        near_out[:, part] = total.astype(BF)
        sent += started(stores(near_out, mine, theirs, c, out_sems))
    waited(sent)


def first_backward_kernel(
    parity, own, other, context_grad, queries_w, own_w, other_w, gains, tables, after, mine, theirs,
    near_q, near_own, near_other, weight_sems, rows, row_sems, near_gains, near_tables, small_sems,
    near_out, out_sems, near_context, context_sem,
):
    del after
    near = (near_q, near_own, near_other)
    row_copies = started(row_loads(own, other, rows, row_sems))
    loads = [started(part) for part in query_loads(queries_w, own_w, other_w, near, weight_sems)]
    small_copies = started(small_loads(gains, tables, near_gains, near_tables, small_sems))
    small_copies += started([pltpu.make_async_copy(context_grad, near_context, context_sem.at[0])])
    waited(row_copies)
    projected = ordered(project_chunks(rows, near, loads), parity[0])
    waited(small_copies)
    grads = attend_back(
        projected, near_context[...], near_gains[...], near_tables[0], near_tables[1], near_tables[2], parity[0]
    )
    grads_out(grads, near, [[]] * STEPS, near_out, mine, theirs, out_sems)


def second_backward_kernel(
    parity, own, other, projected, queries_w, own_w, other_w, output_w, gains, tables, after, mine, theirs,
    near_q, near_own, near_other, weight_sems, rows, row_sems, near_gains, near_tables, small_sems,
    near_out, out_sems, near_output_w, output_sems, near_projected, projected_sem,
):
    del after
    near = (near_q, near_own, near_other)
    row_copies = started(row_loads(own, other, rows, row_sems))
    output_copies = [started(part) for part in output_loads(output_w, near_output_w, output_sems)]
    small_copies = started(small_loads(gains, tables, near_gains, near_tables, small_sems))
    small_copies += started([pltpu.make_async_copy(projected, near_projected, projected_sem.at[0])])
    loads = [started(part) for part in query_loads(queries_w, own_w, other_w, near, weight_sems)]
    waited(row_copies)
    context_grad = context_chunks(rows, near_output_w, output_copies)
    waited(small_copies)
    grads = attend_back(
        near_projected[...], context_grad, near_gains[...], near_tables[0], near_tables[1], near_tables[2], parity[0]
    )
    grads_out(grads, near, loads, near_out, mine, theirs, out_sems)


def far_call(kernel, scalars, arrays, out_shape, scratch, time):
    return pl.pallas_call(
        kernel,
        out_shape=out_shape,
        in_specs=[SCALAR] * len(scalars) + [FAR] * len(arrays),
        out_specs=[FAR] * len(out_shape),
        scratch_shapes=scratch,
        compiler_params=PARAMS,
        cost_estimate=pl.CostEstimate(
            flops=time * 1000000000, bytes_accessed=1000, transcendentals=0
        ),
    )(*scalars, *arrays)


OUTPUT_SCRATCH = [pltpu.VMEM((QUERY, WIDTH), BF), pltpu.SemaphoreType.DMA((STEPS,))]
MAIN_SCRATCH = WEIGHT_SCRATCH + ROW_SCRATCH + SMALL_SCRATCH + OUT_SCRATCH
PROJECTED = jax.ShapeDtypeStruct((ROWS, QUERY + BOTH), BF)
CONTEXT = jax.ShapeDtypeStruct((ROWS, QUERY), jnp.float32)


def run_forward(gathered_rows, weights, small, after):
    arrays = [*gathered_rows, *weights, *small[1:], after]
    scratch = MAIN_SCRATCH + OUTPUT_SCRATCH
    kernel = functools.partial(forward_kernel, len(gathered_rows) == 1)
    return far_call(kernel, small[:1], arrays, [HALF_ROWS] * 2, scratch, 8)


def run_project(rows, weights, small, after):
    scratch = [
        pltpu.VMEM((ROWS, HEAD), jnp.float32),
        pltpu.VMEM(PROJECTED.shape, BF),
        pltpu.SemaphoreType.DMA((2,)),
    ]
    arrays = [rows, *weights[:3], small[2], after]
    return far_call(project_kernel, small[:1], arrays, [PROJECTED], WEIGHT_SCRATCH + ROW_SCRATCH + scratch, 5)[0]


def run_context(own, other, part, output_w, after):
    scratch = [pltpu.VMEM(CONTEXT.shape, CONTEXT.dtype), pltpu.SemaphoreType.DMA((1,))]
    kernel = functools.partial(context_kernel, part)
    arrays = [own, other, output_w, after]
    return far_call(kernel, [], arrays, [CONTEXT], ROW_SCRATCH + OUTPUT_SCRATCH + scratch, 4)[0]


def run_first_backward(own, other, context_grad, weights, small, after):
    scratch = [pltpu.VMEM(CONTEXT.shape, CONTEXT.dtype), pltpu.SemaphoreType.DMA((1,))]
    arrays = [own, other, context_grad, *weights[:3], *small[1:], after]
    outs = [HALF_ROWS] * 2
    return far_call(first_backward_kernel, small[:1], arrays, outs, MAIN_SCRATCH + scratch, 12)


def run_second_backward(own, other, projected, weights, small, after):
    scratch = [pltpu.VMEM(PROJECTED.shape, BF), pltpu.SemaphoreType.DMA((1,))]
    arrays = [own, other, projected, *weights, *small[1:], after]
    scratch = MAIN_SCRATCH + OUTPUT_SCRATCH + scratch
    return far_call(second_backward_kernel, small[:1], arrays, [HALF_ROWS] * 2, scratch, 12)


def mixed(weights, offset, stride, streams):
    return sum(weights[offset + i * stride] * streams[i] for i in range(4))


def normed_rows(scalars, streams, gain):
    total = mixed(scalars, 0, 1, streams.astype(jnp.float32))
    scale = norm_scale(total)
    return (total * scale * gain).astype(BF), total, scale


def out_grad_rows(scalars, grads):
    return mixed(scalars, 4, 1, grads.astype(jnp.float32)).astype(BF)


def front_kernel(scalars, slot, saved, grads, gain, both, combined, scale):
    both[:, :WIDTH], combined[...], row_scale = normed_rows(scalars, saved[slot[0]], gain[...])
    both[:, WIDTH:] = out_grad_rows(scalars, grads[...])
    scale[...] = jnp.broadcast_to(row_scale, scale.shape)


def norm_kernel(scalars, streams, gain, normed):
    normed[...] = normed_rows(scalars, streams[...], gain[...])[0]


def next_norm_kernel(scalars, local, arrived, fresh, gain, normed):
    rows = normed_rows(scalars, fresh[...], gain[...])[0]
    normed[...] = jnp.where(local[0] == 1, rows, arrived[...])


def next_grad_kernel(scalars, local, arrived, loss, out_grad):
    out_grad[...] = jnp.where(local[0] == 1, out_grad_rows(scalars, loss[...]), arrived[...])


def saved_kernel(scalars, slot, saved, gain, normed, combined, scale):
    normed[...], combined[...], row_scale = normed_rows(scalars, saved[1 - slot[0]], gain[...])
    scale[...] = jnp.broadcast_to(row_scale, scale.shape)


def pair_kernel(mine, received, out):
    pair = mine[...].astype(jnp.float32) + received[...].astype(jnp.float32)
    out[...] = pair.astype(out.dtype)


def forward_end_kernel(scalars, landed, streams, out):
    rows = jnp.sum(landed[...].astype(jnp.float32), axis=0)
    streams_f = streams[...].astype(jnp.float32)
    for i in range(4):
        out[i] = (mixed(scalars, 8 + 4 * i, 1, streams_f) + scalars[4 + i] * rows).astype(out.dtype)


def forward_next_kernel(scalars, following, landed, streams, next_gain, out, normed):
    forward_end_kernel(scalars, landed, streams, out)
    normed[...] = normed_rows(following, out[...], next_gain[...])[0]


def backward_next_kernel(scalars, preceding, landed, grads, gain, combined, scale, out, out_grad):
    backward_end_kernel(scalars, landed, grads, gain, combined, scale, out)
    out_grad[...] = out_grad_rows(preceding, out[...])


def backward_end_kernel(scalars, landed, grads, gain, combined, scale, out):
    weighted = jnp.sum(landed[...].astype(jnp.float32), axis=0) * gain[...]
    row_scale = scale[:, :1]
    inner = jnp.mean(weighted * combined[...], axis=-1, keepdims=True)
    combined_grad = row_scale * weighted - combined[...] * (row_scale * row_scale * row_scale * inner)
    grads_f = grads[...].astype(jnp.float32)
    for j in range(4):
        out[j] = (mixed(scalars, 8 + j, 4, grads_f) + scalars[j] * combined_grad).astype(out.dtype)


def plain(kernel, scalars, arrays, outs, after=None):
    n, m, k = len(scalars), len(arrays), len(outs)
    extra = [] if after is None else [after]
    e = len(extra)

    def body(*refs):
        far_in, far_out = refs[n : n + m], refs[n + m + e : n + m + e + k]
        rest = refs[n + m + e + k :]
        near_in, near_out, sems, out_sems = rest[:m], rest[m : m + k], rest[m + k], rest[m + k + 1]
        waited(
            started([pltpu.make_async_copy(far_in[i], near_in[i], sems.at[i]) for i in range(m)])
        )
        kernel(*refs[:n], *near_in, *near_out)
        sent = []
        for i in range(k):
            if outs[i][2]:
                for chip in range(8):
                    sent.append(
                        pltpu.make_async_copy(near_out[i], far_out[i].at[chip], out_sems.at[i, chip])
                    )
            else:
                sent.append(pltpu.make_async_copy(near_out[i], far_out[i], out_sems.at[i, 0]))
        waited(started(sent))

    shapes = [((8,) if out[2] else ()) + out[0] for out in outs]
    return pl.pallas_call(
        body,
        out_shape=[jax.ShapeDtypeStruct(shape, out[1]) for shape, out in zip(shapes, outs)],
        in_specs=[SCALAR] * n + [FAR] * (m + e),
        out_specs=[FAR] * k,
        scratch_shapes=[pltpu.VMEM(array.shape, array.dtype) for array in arrays]
        + [pltpu.VMEM(out[0], out[1]) for out in outs]
        + [pltpu.SemaphoreType.DMA((m,)), pltpu.SemaphoreType.DMA((k, 8))],
        compiler_params=PARAMS,
        cost_estimate=pl.CostEstimate(flops=2500000000, bytes_accessed=1000, transcendentals=0),
    )(*scalars, *arrays, *extra)


def after(value, *events):
    return lax.optimization_barrier((value, *events))[0]


def landed_rows(copies):
    own = lax.all_to_all(copies, "tensor", 0, 0, axis_index_groups=GROUPS, tiled=True)
    return own.reshape(HALF, -1)


def paired(mine, received, event):
    return plain(pair_kernel, [], [mine, received], [(mine.shape, mine.dtype, False)], event)[0]


def scattered(pair):
    return lax.all_to_all(
        pair.reshape(8, LOCAL, -1), "tensor", 0, 0, axis_index_groups=GROUPS, tiled=True
    )


def on_device(
    entering_streams,
    entering_grads,
    fresh_streams,
    loss_grads,
    stashed,
    slot_order,
    q_weight,
    kv_weight,
    out_weight,
    norm_gain,
    head_gains,
    stream_in,
    stream_out,
    stream_mix,
):
    section = lax.axis_index("section")
    parity = lax.axis_index("tensor") % 2
    partner = (section + 8) % 16
    queries_w, output_w = q_weight[0], out_weight[0]
    gain, gains = norm_gain[0], head_gains[0]
    mix_in, mix_out, mix = stream_in[0], stream_out[0], stream_mix[0]
    bf16, f32 = jnp.bfloat16, jnp.float32

    tables = jnp.where(parity == 0, jnp.asarray(TABLES[0]), jnp.asarray(TABLES[1]))

    own_w = jnp.swapaxes(kv_weight[0], 1, 2).reshape(HEAD, -1)
    other_w = other_core(own_w)
    weights = (queries_w, own_w, other_w, output_w)
    small = (parity[None].astype(jnp.int32), gains, tables)
    gain_row, mix_flat = gain[None], mix.reshape(16)
    row_shape, streams_shape = (LOCAL, WIDTH), (4, LOCAL, WIDTH)
    row, copied = (row_shape, bf16, False), (row_shape, bf16, True)
    streams_out = (streams_shape, bf16, False)
    state_outs = [(row_shape, f32, False), ((LOCAL, HEAD), f32, False)]

    scalars = jnp.concatenate([mix_in, mix_out, mix_flat])
    saved = to_partner(stashed[:, 0])
    forward_now, backward_now = entering_streams[0], entering_grads[0]
    params = jnp.concatenate([gain, scalars, jnp.zeros((104,), f32)])[None]
    params = shifted(params, -1)
    preceding = shifted(scalars, 1)
    at_start = (section == 0).astype(jnp.int32)[None]
    at_end = (section == 15).astype(jnp.int32)[None]
    slot = slot_order[section, 0][None]
    normed = plain(norm_kernel, [scalars], [forward_now, gain_row], [copied])[0]
    normed, saved, params, preceding = lax.optimization_barrier((normed, saved, params, preceding))
    next_gain, following = params[:, :WIDTH], params[0, WIDTH : WIDTH + 24]
    own = landed_rows(normed)
    other = other_core(own)

    both_out = ((LOCAL, 2 * WIDTH), bf16, True)
    both, *first_state = plain(
        front_kernel, [scalars, slot], [saved, backward_now, gain_row], [both_out] + state_outs, normed
    )
    both_own = landed_rows(both)

    forward_partial = run_forward([own, other], weights, small, both)
    forward_received = other_core(forward_partial[1])
    both_own = after(both_own, forward_partial[0])
    both_other = other_core(both_own)
    saved_normed, *second_state = plain(
        saved_kernel, [scalars, slot], [saved, gain_row], [row] + state_outs, forward_partial[0]
    )
    saved_rows = lax.all_gather(saved_normed, "tensor", axis=0, tiled=True)
    forward_pair = paired(forward_partial[0], forward_received, saved_normed)
    landed = scattered(forward_pair)

    evicted_first = to_partner(forward_now)
    both_other = after(both_other, forward_pair)
    context_grad = run_context(both_own, both_other, 1, output_w, evicted_first)
    backward_partial = run_first_backward(both_own, both_other, context_grad, weights, small, context_grad)
    backward_received = other_core(backward_partial[1])
    forward_out, next_normed = plain(
        forward_next_kernel,
        [scalars, following],
        [landed, forward_now, next_gain],
        [streams_out, row],
        backward_partial[0],
    )
    arrived = shifted(next_normed, 1)

    backward_pair = paired(backward_partial[0], backward_received, forward_out)
    landed = scattered(after(backward_pair, arrived))
    arrived = after(arrived, backward_pair)
    normed_copies = plain(
        next_norm_kernel, [scalars, at_start], [arrived, fresh_streams[0], gain_row], [copied]
    )[0]
    projected = run_project(saved_rows, weights, small, normed_copies)
    own = landed_rows(after(normed_copies, projected))
    backward_out, next_grad = plain(
        backward_next_kernel,
        [scalars, preceding],
        [landed, backward_now, gain_row, *first_state],
        [streams_out, row],
        projected,
    )
    arrived = shifted(next_grad, -1)

    grad_copies = plain(
        next_grad_kernel, [scalars, at_end], [arrived, loss_grads[0]], [copied]
    )[0]
    grad_own = landed_rows(grad_copies)
    own = after(own, arrived)
    other = other_core(own)
    forward_sent = after(forward_out, own)
    from_previous = shifted(forward_sent, 1)
    forward_partial = run_forward([own, other], weights, small, grad_copies)
    forward_received = other_core(forward_partial[1])
    own = after(grad_own, forward_partial[0])
    other = other_core(own)
    from_following = shifted(after(backward_out, own), -1)
    forward_pair = paired(forward_partial[0], forward_received, grad_copies)
    landed_forward = scattered(after(forward_pair, own))
    backward_partial = run_second_backward(own, other, projected, weights, small, forward_pair)
    backward_pair = paired(backward_partial[0], other_core(backward_partial[1]), from_following)
    landed_backward = scattered(backward_pair)
    from_previous = after(from_previous, backward_partial[0])
    forward_now = jnp.where(section == 0, fresh_streams[0], from_previous)
    evicted_second = to_partner(forward_now)
    backward_now = jnp.where(section == 15, loss_grads[0], from_following)
    forward_out = plain(
        forward_end_kernel, [scalars], [landed_forward, forward_now], [streams_out], backward_pair
    )[0]
    backward_out = plain(
        backward_end_kernel,
        [scalars],
        [landed_backward, backward_now, gain_row, *second_state],
        [streams_out],
        forward_out,
    )[0]
    evicted = jnp.stack([evicted_first, evicted_second])
    return (forward_out[None], backward_out[None], evicted[:, None])


def solution(mesh):
    return jax.shard_map(
        on_device,
        mesh=mesh,
        in_specs=(
            P("section", None, "tensor", None),
            P("section", None, "tensor", None),
            P(None, None, "tensor", None),
            P(None, None, "tensor", None),
            P(None, "section", None, "tensor", None),
            P(),
            P("section", None, "tensor"),
            P("section", None, None, "tensor"),
            P("section", "tensor", None),
            P("section", None),
            P("section", None, None),
            P("section", None),
            P("section", None),
            P("section", None, None),
        ),
        out_specs=(
            P("section", None, "tensor", None),
            P("section", None, "tensor", None),
            P(None, "section", None, "tensor", None),
        ),
        check_vma=False,
    )
```

```python
import functools
import math

import jax
import jax.numpy as jnp
import numpy as np
from jax import lax
from jax.experimental import pallas as pl
from jax.experimental.pallas import tpu as pltpu
from jax.sharding import PartitionSpec as P

EPSILON = 1e-06
ROPE_BASE = 1000000.0
ROWS = 128
LOCAL = 8
HEAD = 128
WIDTH = 5120
CHUNK = 2560
STEPS = WIDTH // CHUNK
QUERY = 384
BOTH = 256
GROUPS = [[core + 2 * chip for chip in range(8)] for core in range(2)]


def other_core(value):
    return lax.ppermute(value, "tensor", [(i, i ^ 1) for i in range(16)])


def to_partner(value):
    return lax.ppermute(value, "section", [(i, i ^ 8) for i in range(16)])


def shifted(value, by):
    return lax.ppermute(value, "section", [(i, (i + by) % 16) for i in range(16)])


def token_order(parity):
    own = [2 * chip + parity for chip in range(8)]
    other = [2 * chip + 1 - parity for chip in range(8)]
    return np.concatenate([np.arange(LOCAL) + LOCAL * block for block in own + other])


def tables_of(order):
    half = HEAD // 2
    frequency = np.float32(ROPE_BASE) ** (-np.arange(half, dtype=np.float32) / np.float32(half))
    angles = order.astype(np.float32)[:, None] * frequency[None, :]
    cosine, sine = np.cos(angles), np.sin(angles)
    mask = np.where(order[:, None] >= order[None, :], 0.0, -1e30)
    turn = order[:, None] == np.arange(ROWS)[None, :]
    planes = [np.concatenate([cosine, cosine], 1), np.concatenate([-sine, sine], 1), mask, turn]
    return np.stack(planes).astype(np.float32)


TABLES = np.stack([tables_of(token_order(0)), tables_of(token_order(1))])


def dot(left, right):
    return jnp.dot(left, right, preferred_element_type=jnp.float32)


def dot_nt(left, right):
    return lax.dot_general(left, right, (((1,), (1,)), ((), ())), preferred_element_type=jnp.float32)


def dot_tn(left, right):
    return lax.dot_general(left, right, (((0,), (0,)), ((), ())), preferred_element_type=jnp.float32)


def rope(values, cosine, sine):
    return values * cosine + pltpu.roll(values, HEAD // 2, 1) * sine


def rope_back(grads, cosine, sine):
    return grads * cosine - pltpu.roll(grads, HEAD // 2, 1) * sine


def norm_scale(values):
    return lax.rsqrt(jnp.mean(values * values, axis=-1, keepdims=True) + EPSILON)


def head_back(grads, values, scale, gain):
    weighted = grads * gain
    inner = jnp.mean(values * weighted, axis=-1, keepdims=True)
    return scale * weighted - values * (scale * scale * scale * inner)


def softmax_of(query_head, key_head, mask):
    scores = dot_nt(query_head, key_head) * (1.0 / math.sqrt(HEAD)) + mask
    scores = scores - jnp.max(scores, axis=-1, keepdims=True)
    weights = jnp.exp(scores)
    return weights / jnp.sum(weights, axis=-1, keepdims=True)


def joined(own, other, parity):
    first = jnp.where(parity == 0, own, other)
    second = jnp.where(parity == 0, other, own)
    return jnp.concatenate([first, second], axis=1)


def ordered(total, parity):
    own, other = total[:, QUERY : QUERY + HEAD], total[:, QUERY + HEAD :]
    half = HEAD // 2
    keys = joined(own[:, :half], other[:, :half], parity)
    values = joined(own[:, half:], other[:, half:], parity)
    return jnp.concatenate([total[:, :QUERY], keys, values], axis=1).astype(jnp.bfloat16)


def attend(projected, gains, cosine, sine, mask):
    bf16, f32 = jnp.bfloat16, jnp.float32
    keys = projected[:, QUERY : QUERY + HEAD].astype(f32)
    key_head = rope(keys * norm_scale(keys) * gains[1:2], cosine, sine).astype(bf16)
    values = projected[:, QUERY + HEAD :]
    context = []
    for head in range(QUERY // HEAD):
        queries = projected[:, head * HEAD : (head + 1) * HEAD].astype(f32)
        query_head = rope(queries * norm_scale(queries) * gains[0:1], cosine, sine).astype(bf16)
        weights = softmax_of(query_head, key_head, mask)
        context.append(dot(weights.astype(bf16), values).astype(bf16))
    return jnp.concatenate(context, axis=1)


def attend_back(projected, context_grad, gains, cosine, sine, mask, parity):
    bf16, f32 = jnp.bfloat16, jnp.float32
    root = 1.0 / math.sqrt(HEAD)
    keys = projected[:, QUERY : QUERY + HEAD].astype(f32)
    key_scale = norm_scale(keys)
    key_head = rope(keys * key_scale * gains[1:2], cosine, sine).astype(bf16)
    values = projected[:, QUERY + HEAD :]
    query_grads = []
    key_total = jnp.zeros((ROWS, HEAD), f32)
    value_total = jnp.zeros((ROWS, HEAD), f32)
    for head in range(QUERY // HEAD):
        queries = projected[:, head * HEAD : (head + 1) * HEAD].astype(f32)
        query_scale = norm_scale(queries)
        query_head = rope(queries * query_scale * gains[0:1], cosine, sine).astype(bf16)
        weights = softmax_of(query_head, key_head, mask)
        upstream = context_grad[:, head * HEAD : (head + 1) * HEAD].astype(bf16)
        value_total = value_total + dot_tn(weights.astype(bf16), upstream)
        weights_grad = dot_nt(upstream, values).astype(bf16).astype(f32)
        inner = jnp.sum(weights * weights_grad, axis=-1, keepdims=True)
        scores_grad = (weights * (weights_grad - inner) * root).astype(bf16)
        key_total = key_total + dot_tn(scores_grad, query_head)
        turned = rope_back(dot(scores_grad, key_head), cosine, sine)
        query_grads.append(head_back(turned, queries, query_scale, gains[0:1]).astype(bf16))
    key_grad = head_back(rope_back(key_total, cosine, sine), keys, key_scale, gains[1:2])
    half = HEAD // 2
    own = joined(key_grad[:, :half], value_total[:, :half], 0)
    other = joined(key_grad[:, half:], value_total[:, half:], 0)
    first = jnp.where(parity == 0, own, other)
    second = jnp.where(parity == 0, other, own)
    return jnp.concatenate(query_grads, axis=1), first.astype(bf16), second.astype(bf16)


PARAMS = pltpu.CompilerParams(vmem_limit_bytes=62 * 2**20)
SCALAR = pl.BlockSpec(memory_space=pltpu.SMEM)
FAR = pl.BlockSpec(memory_space=pl.ANY)
HALF = ROWS // 2
HALF_ROWS = jax.ShapeDtypeStruct((HALF, WIDTH), jnp.bfloat16)
BF = jnp.bfloat16


def started(copies):
    for copy in copies:
        copy.start()
    return copies


def waited(copies):
    for copy in copies:
        copy.wait()


def columns(chunk):
    return pl.ds(chunk * CHUNK, CHUNK)


def query_loads(queries_w, own_w, other_w, near, sems):
    near_q, near_own, near_other = near
    return [
        [
            pltpu.make_async_copy(
                queries_w.at[columns(c), :], near_q.at[columns(c), :], sems.at[c, 0]
            ),
            pltpu.make_async_copy(own_w.at[:, columns(c)], near_own.at[:, columns(c)], sems.at[c, 1]),
            pltpu.make_async_copy(
                other_w.at[:, columns(c)], near_other.at[:, columns(c)], sems.at[c, 2]
            ),
        ]
        for c in range(STEPS)
    ]


def output_loads(output_w, near, sems):
    return [
        [pltpu.make_async_copy(output_w.at[:, columns(c)], near.at[:, columns(c)], sems.at[c])]
        for c in range(STEPS)
    ]


def row_loads(own, other, rows, sems, part=0):
    if other is None:
        return [pltpu.make_async_copy(own, rows, sems.at[0])]
    source = pl.ds(part * WIDTH, WIDTH)
    return [
        pltpu.make_async_copy(own.at[:, source], rows.at[pl.ds(0, HALF), :], sems.at[0]),
        pltpu.make_async_copy(other.at[:, source], rows.at[pl.ds(HALF, HALF), :], sems.at[1]),
    ]


def stores(near, mine, theirs, c, sems):
    return [
        pltpu.make_async_copy(
            near.at[pl.ds(HALF, HALF), columns(c)], theirs.at[:, columns(c)], sems.at[c, 0]
        ),
        pltpu.make_async_copy(
            near.at[pl.ds(0, HALF), columns(c)], mine.at[:, columns(c)], sems.at[c, 1]
        ),
    ]


def project_chunks(rows, near, loads):
    near_q, near_own, near_other = near
    queries = own = other = 0.0
    for c in range(STEPS):
        waited(loads[c])
        part = rows[:, c * CHUNK : (c + 1) * CHUNK]
        queries += dot(part, near_q[c * CHUNK : (c + 1) * CHUNK, :])
        own += dot_nt(part, near_own[:, c * CHUNK : (c + 1) * CHUNK])
        other += dot_nt(part, near_other[:, c * CHUNK : (c + 1) * CHUNK])
    return jnp.concatenate([queries, own, other], axis=1)


WEIGHT_SCRATCH = [
    pltpu.VMEM((WIDTH, QUERY), BF),
    pltpu.VMEM((HEAD, WIDTH), BF),
    pltpu.VMEM((HEAD, WIDTH), BF),
    pltpu.SemaphoreType.DMA((STEPS, 3)),
]
ROW_SCRATCH = [pltpu.VMEM((ROWS, WIDTH), BF), pltpu.SemaphoreType.DMA((2,))]
SMALL_SCRATCH = [
    pltpu.VMEM((2, HEAD), jnp.float32),
    pltpu.VMEM((4, ROWS, HEAD), jnp.float32),
    pltpu.SemaphoreType.DMA((2,)),
]
OUT_SCRATCH = [pltpu.VMEM((ROWS, WIDTH), BF), pltpu.SemaphoreType.DMA((STEPS, 2))]


def small_loads(gains, tables, near_gains, near_tables, sems):
    return [
        pltpu.make_async_copy(gains, near_gains, sems.at[0]),
        pltpu.make_async_copy(tables, near_tables, sems.at[1]),
    ]


def forward_kernel(
    turned, parity, *refs
):
    own, other = refs[0], None if turned else refs[1]
    queries_w, own_w, other_w, output_w, gains, tables, _, *rest = refs[1 if turned else 2 :]
    mine, theirs, near_q, near_own, near_other, weight_sems, rows, row_sems = rest[:8]
    near_gains, near_tables, small_sems, near_out, out_sems, near_output_w, output_sems = rest[8:15]
    near = (near_q, near_own, near_other)
    row_copies = started(row_loads(own, other, rows, row_sems))
    loads = [started(part) for part in query_loads(queries_w, own_w, other_w, near, weight_sems)]
    small_copies = started(small_loads(gains, tables, near_gains, near_tables, small_sems))
    output_copies = [started(part) for part in output_loads(output_w, near_output_w, output_sems)]
    waited(row_copies)
    projected = ordered(project_chunks(rows, near, loads), parity[0])
    waited(small_copies)
    if turned:
        projected = dot(near_tables[3].astype(BF), projected).astype(BF)
    context = attend(projected, near_gains[...], near_tables[0], near_tables[1], near_tables[2])
    sent = []
    for c in range(STEPS):
        waited(output_copies[c])
        part = dot(context, near_output_w[:, c * CHUNK : (c + 1) * CHUNK])
        near_out[:, c * CHUNK : (c + 1) * CHUNK] = part.astype(BF)
        sent += started(stores(near_out, mine, theirs, c, out_sems))
    waited(sent)


def project_kernel(
    parity, own, other, queries_w, own_w, other_w, after, out,
    near_q, near_own, near_other, weight_sems, rows, row_sems, near_out, sems,
):
    del after
    near = (near_q, near_own, near_other)
    row_copies = started(row_loads(own, other, rows, row_sems, 2))
    loads = [started(part) for part in query_loads(queries_w, own_w, other_w, near, weight_sems)]
    waited(row_copies)
    projected = ordered(project_chunks(rows, near, loads), parity[0])
    near_out[...] = projected
    waited(started([pltpu.make_async_copy(near_out, out, sems.at[0])]))


def context_kernel(
    part, own, other, output_w, after, out, rows, row_sems, near_output_w, output_sems, near_out, sems
):
    del after
    row_copies = started(row_loads(own, other, rows, row_sems, part))
    output_copies = [started(chunk) for chunk in output_loads(output_w, near_output_w, output_sems)]
    waited(row_copies)
    near_out[...] = context_chunks(rows, near_output_w, output_copies)
    waited(started([pltpu.make_async_copy(near_out, out, sems.at[0])]))


def context_chunks(rows, near_output_w, output_copies):
    context_grad = 0.0
    for c in range(STEPS):
        waited(output_copies[c])
        part = slice(c * CHUNK, (c + 1) * CHUNK)
        context_grad += dot_nt(rows[:, part], near_output_w[:, part])
    return context_grad


def grads_out(grads, near, loads, near_out, mine, theirs, out_sems):
    query_grad, own_grad, other_grad = grads
    near_q, near_own, near_other = near
    sent = []
    for c in range(STEPS):
        waited(loads[c])
        part = slice(c * CHUNK, (c + 1) * CHUNK)
        total = dot_nt(query_grad, near_q[part, :])
        total = total + dot(own_grad, near_own[:, part]) + dot(other_grad, near_other[:, part])
        near_out[:, part] = total.astype(BF)
        sent += started(stores(near_out, mine, theirs, c, out_sems))
    waited(sent)


def first_backward_kernel(
    parity, own, other, context_grad, queries_w, own_w, other_w, gains, tables, after, mine, theirs,
    near_q, near_own, near_other, weight_sems, rows, row_sems, near_gains, near_tables, small_sems,
    near_out, out_sems, near_context, context_sem,
):
    del after
    near = (near_q, near_own, near_other)
    row_copies = started(row_loads(own, other, rows, row_sems))
    loads = [started(part) for part in query_loads(queries_w, own_w, other_w, near, weight_sems)]
    small_copies = started(small_loads(gains, tables, near_gains, near_tables, small_sems))
    small_copies += started([pltpu.make_async_copy(context_grad, near_context, context_sem.at[0])])
    waited(row_copies)
    projected = ordered(project_chunks(rows, near, loads), parity[0])
    waited(small_copies)
    grads = attend_back(
        projected, near_context[...], near_gains[...], near_tables[0], near_tables[1], near_tables[2], parity[0]
    )
    grads_out(grads, near, [[]] * STEPS, near_out, mine, theirs, out_sems)


def second_backward_kernel(
    parity, own, other, projected, queries_w, own_w, other_w, output_w, gains, tables, after, mine, theirs,
    near_q, near_own, near_other, weight_sems, rows, row_sems, near_gains, near_tables, small_sems,
    near_out, out_sems, near_output_w, output_sems, near_projected, projected_sem,
):
    del after
    near = (near_q, near_own, near_other)
    row_copies = started(row_loads(own, other, rows, row_sems))
    output_copies = [started(part) for part in output_loads(output_w, near_output_w, output_sems)]
    small_copies = started(small_loads(gains, tables, near_gains, near_tables, small_sems))
    small_copies += started([pltpu.make_async_copy(projected, near_projected, projected_sem.at[0])])
    loads = [started(part) for part in query_loads(queries_w, own_w, other_w, near, weight_sems)]
    waited(row_copies)
    context_grad = context_chunks(rows, near_output_w, output_copies)
    waited(small_copies)
    grads = attend_back(
        near_projected[...], context_grad, near_gains[...], near_tables[0], near_tables[1], near_tables[2], parity[0]
    )
    grads_out(grads, near, loads, near_out, mine, theirs, out_sems)


def far_call(kernel, scalars, arrays, out_shape, scratch, time):
    return pl.pallas_call(
        kernel,
        out_shape=out_shape,
        in_specs=[SCALAR] * len(scalars) + [FAR] * len(arrays),
        out_specs=[FAR] * len(out_shape),
        scratch_shapes=scratch,
        compiler_params=PARAMS,
        cost_estimate=pl.CostEstimate(
            flops=time * 1000000000, bytes_accessed=1000, transcendentals=0
        ),
    )(*scalars, *arrays)


OUTPUT_SCRATCH = [pltpu.VMEM((QUERY, WIDTH), BF), pltpu.SemaphoreType.DMA((STEPS,))]
MAIN_SCRATCH = WEIGHT_SCRATCH + ROW_SCRATCH + SMALL_SCRATCH + OUT_SCRATCH
PROJECTED = jax.ShapeDtypeStruct((ROWS, QUERY + BOTH), BF)
CONTEXT = jax.ShapeDtypeStruct((ROWS, QUERY), jnp.float32)


def run_forward(gathered_rows, weights, small, after):
    arrays = [*gathered_rows, *weights, *small[1:], after]
    scratch = MAIN_SCRATCH + OUTPUT_SCRATCH
    kernel = functools.partial(forward_kernel, len(gathered_rows) == 1)
    return far_call(kernel, small[:1], arrays, [HALF_ROWS] * 2, scratch, 8)


def run_project(own, other, weights, small, after):
    scratch = [pltpu.VMEM(PROJECTED.shape, BF), pltpu.SemaphoreType.DMA((1,))]
    arrays = [own, other, *weights[:3], after]
    scratch = WEIGHT_SCRATCH + ROW_SCRATCH + scratch
    return far_call(project_kernel, small[:1], arrays, [PROJECTED], scratch, 5)[0]


def run_context(own, other, part, output_w, after):
    scratch = [pltpu.VMEM(CONTEXT.shape, CONTEXT.dtype), pltpu.SemaphoreType.DMA((1,))]
    kernel = functools.partial(context_kernel, part)
    arrays = [own, other, output_w, after]
    return far_call(kernel, [], arrays, [CONTEXT], ROW_SCRATCH + OUTPUT_SCRATCH + scratch, 4)[0]


def run_first_backward(own, other, context_grad, weights, small, after):
    scratch = [pltpu.VMEM(CONTEXT.shape, CONTEXT.dtype), pltpu.SemaphoreType.DMA((1,))]
    arrays = [own, other, context_grad, *weights[:3], *small[1:], after]
    outs = [HALF_ROWS] * 2
    return far_call(first_backward_kernel, small[:1], arrays, outs, MAIN_SCRATCH + scratch, 12)


def run_second_backward(own, other, projected, weights, small, after):
    scratch = [pltpu.VMEM(PROJECTED.shape, BF), pltpu.SemaphoreType.DMA((1,))]
    arrays = [own, other, projected, *weights, *small[1:], after]
    scratch = MAIN_SCRATCH + OUTPUT_SCRATCH + scratch
    return far_call(second_backward_kernel, small[:1], arrays, [HALF_ROWS] * 2, scratch, 12)


def mixed(weights, offset, stride, streams):
    return sum(weights[offset + i * stride] * streams[i] for i in range(4))


def normed_rows(scalars, streams, gain):
    total = mixed(scalars, 0, 1, streams.astype(jnp.float32))
    scale = norm_scale(total)
    return (total * scale * gain).astype(BF), total, scale


def out_grad_rows(scalars, grads):
    return mixed(scalars, 4, 1, grads.astype(jnp.float32)).astype(BF)


def front_kernel(scalars, slot, saved, grads, gain, every, *states):
    for tick in range(2):
        combined, scale = states[2 * tick : 2 * tick + 2]
        chosen = slot[0] if tick == 0 else 1 - slot[0]
        normed, combined[...], row_scale = normed_rows(scalars, saved[chosen], gain[...])
        every[:, 2 * tick * WIDTH : (2 * tick + 1) * WIDTH] = normed
        scale[...] = jnp.broadcast_to(row_scale, scale.shape)
    every[:, WIDTH : 2 * WIDTH] = out_grad_rows(scalars, grads[...])


def norm_kernel(scalars, streams, gain, normed):
    normed[...] = normed_rows(scalars, streams[...], gain[...])[0]


def next_norm_kernel(scalars, local, arrived, fresh, gain, normed):
    rows = normed_rows(scalars, fresh[...], gain[...])[0]
    normed[...] = jnp.where(local[0] == 1, rows, arrived[...])


def next_grad_kernel(scalars, local, arrived, loss, out_grad):
    out_grad[...] = jnp.where(local[0] == 1, out_grad_rows(scalars, loss[...]), arrived[...])


def pair_kernel(mine, received, out):
    pair = mine[...].astype(jnp.float32) + received[...].astype(jnp.float32)
    out[...] = pair.astype(out.dtype)


def forward_end_kernel(scalars, landed, streams, out):
    rows = jnp.sum(landed[...].astype(jnp.float32), axis=0)
    streams_f = streams[...].astype(jnp.float32)
    for i in range(4):
        out[i] = (mixed(scalars, 8 + 4 * i, 1, streams_f) + scalars[4 + i] * rows).astype(out.dtype)


def forward_next_kernel(scalars, following, landed, streams, next_gain, out, normed):
    forward_end_kernel(scalars, landed, streams, out)
    normed[...] = normed_rows(following, out[...], next_gain[...])[0]


def backward_next_kernel(scalars, preceding, landed, grads, gain, combined, scale, out, out_grad):
    backward_end_kernel(scalars, landed, grads, gain, combined, scale, out)
    out_grad[...] = out_grad_rows(preceding, out[...])


def backward_end_kernel(scalars, landed, grads, gain, combined, scale, out):
    weighted = jnp.sum(landed[...].astype(jnp.float32), axis=0) * gain[...]
    row_scale = scale[:, :1]
    inner = jnp.mean(weighted * combined[...], axis=-1, keepdims=True)
    combined_grad = row_scale * weighted - combined[...] * (row_scale * row_scale * row_scale * inner)
    grads_f = grads[...].astype(jnp.float32)
    for j in range(4):
        out[j] = (mixed(scalars, 8 + j, 4, grads_f) + scalars[j] * combined_grad).astype(out.dtype)


def plain(kernel, scalars, arrays, outs, after=None):
    n, m, k = len(scalars), len(arrays), len(outs)
    extra = [] if after is None else [after]
    e = len(extra)

    def body(*refs):
        far_in, far_out = refs[n : n + m], refs[n + m + e : n + m + e + k]
        rest = refs[n + m + e + k :]
        near_in, near_out, sems, out_sems = rest[:m], rest[m : m + k], rest[m + k], rest[m + k + 1]
        waited(
            started([pltpu.make_async_copy(far_in[i], near_in[i], sems.at[i]) for i in range(m)])
        )
        kernel(*refs[:n], *near_in, *near_out)
        sent = []
        for i in range(k):
            if outs[i][2]:
                for chip in range(8):
                    sent.append(
                        pltpu.make_async_copy(near_out[i], far_out[i].at[chip], out_sems.at[i, chip])
                    )
            else:
                sent.append(pltpu.make_async_copy(near_out[i], far_out[i], out_sems.at[i, 0]))
        waited(started(sent))

    shapes = [((8,) if out[2] else ()) + out[0] for out in outs]
    return pl.pallas_call(
        body,
        out_shape=[jax.ShapeDtypeStruct(shape, out[1]) for shape, out in zip(shapes, outs)],
        in_specs=[SCALAR] * n + [FAR] * (m + e),
        out_specs=[FAR] * k,
        scratch_shapes=[pltpu.VMEM(array.shape, array.dtype) for array in arrays]
        + [pltpu.VMEM(out[0], out[1]) for out in outs]
        + [pltpu.SemaphoreType.DMA((m,)), pltpu.SemaphoreType.DMA((k, 8))],
        compiler_params=PARAMS,
        cost_estimate=pl.CostEstimate(flops=2500000000, bytes_accessed=1000, transcendentals=0),
    )(*scalars, *arrays, *extra)


def after(value, *events):
    return lax.optimization_barrier((value, *events))[0]


def landed_rows(copies):
    own = lax.all_to_all(copies, "tensor", 0, 0, axis_index_groups=GROUPS, tiled=True)
    return own.reshape(HALF, -1)


def paired(mine, received, event):
    return plain(pair_kernel, [], [mine, received], [(mine.shape, mine.dtype, False)], event)[0]


def scattered(pair):
    return lax.all_to_all(
        pair.reshape(8, LOCAL, -1), "tensor", 0, 0, axis_index_groups=GROUPS, tiled=True
    )


def on_device(
    entering_streams,
    entering_grads,
    fresh_streams,
    loss_grads,
    stashed,
    slot_order,
    q_weight,
    kv_weight,
    out_weight,
    norm_gain,
    head_gains,
    stream_in,
    stream_out,
    stream_mix,
):
    section = lax.axis_index("section")
    parity = lax.axis_index("tensor") % 2
    partner = (section + 8) % 16
    queries_w, output_w = q_weight[0], out_weight[0]
    gain, gains = norm_gain[0], head_gains[0]
    mix_in, mix_out, mix = stream_in[0], stream_out[0], stream_mix[0]
    bf16, f32 = jnp.bfloat16, jnp.float32

    tables = jnp.where(parity == 0, jnp.asarray(TABLES[0]), jnp.asarray(TABLES[1]))

    own_w = jnp.swapaxes(kv_weight[0], 1, 2).reshape(HEAD, -1)
    other_w = other_core(own_w)
    weights = (queries_w, own_w, other_w, output_w)
    small = (parity[None].astype(jnp.int32), gains, tables)
    gain_row, mix_flat = gain[None], mix.reshape(16)
    row_shape, streams_shape = (LOCAL, WIDTH), (4, LOCAL, WIDTH)
    row, copied = (row_shape, bf16, False), (row_shape, bf16, True)
    streams_out = (streams_shape, bf16, False)
    state_outs = [(row_shape, f32, False), ((LOCAL, HEAD), f32, False)]

    scalars = jnp.concatenate([mix_in, mix_out, mix_flat])
    saved = to_partner(stashed[:, 0])
    forward_now, backward_now = entering_streams[0], entering_grads[0]
    params = jnp.concatenate([gain, scalars, jnp.zeros((104,), f32)])[None]
    params = shifted(params, -1)
    preceding = shifted(scalars, 1)
    at_start = (section == 0).astype(jnp.int32)[None]
    at_end = (section == 15).astype(jnp.int32)[None]
    slot = slot_order[section, 0][None]
    normed = plain(norm_kernel, [scalars], [forward_now, gain_row], [copied])[0]
    normed, saved, params, preceding = lax.optimization_barrier((normed, saved, params, preceding))
    next_gain, following = params[:, :WIDTH], params[0, WIDTH : WIDTH + 24]
    own = landed_rows(normed)
    other = other_core(own)

    both_out = ((LOCAL, 3 * WIDTH), bf16, True)
    both, *states = plain(
        front_kernel, [scalars, slot], [saved, backward_now, gain_row], [both_out] + state_outs * 2, normed
    )
    first_state, second_state = states[:2], states[2:]
    both_own = landed_rows(both)

    forward_partial = run_forward([own, other], weights, small, both)
    forward_received = other_core(forward_partial[1])
    forward_pair = paired(forward_partial[0], forward_received, forward_partial[0])
    evicted_first = to_partner(forward_now)
    both_own = after(both_own, forward_pair, evicted_first)
    both_other = other_core(both_own)
    landed = scattered(forward_pair)

    context_grad = run_context(both_own, both_other, 1, output_w, evicted_first)
    backward_partial = run_first_backward(both_own, both_other, context_grad, weights, small, context_grad)
    backward_received = other_core(backward_partial[1])
    forward_out, next_normed = plain(
        forward_next_kernel,
        [scalars, following],
        [landed, forward_now, next_gain],
        [streams_out, row],
        backward_partial[0],
    )
    arrived = shifted(next_normed, 1)

    backward_pair = paired(backward_partial[0], backward_received, forward_out)
    landed = scattered(after(backward_pair, arrived))
    arrived = after(arrived, backward_pair)
    normed_copies = plain(
        next_norm_kernel, [scalars, at_start], [arrived, fresh_streams[0], gain_row], [copied]
    )[0]
    projected = run_project(both_own, both_other, weights, small, normed_copies)
    own = landed_rows(after(normed_copies, projected))
    backward_out, next_grad = plain(
        backward_next_kernel,
        [scalars, preceding],
        [landed, backward_now, gain_row, *first_state],
        [streams_out, row],
        projected,
    )
    arrived = shifted(next_grad, -1)

    grad_copies = plain(
        next_grad_kernel, [scalars, at_end], [arrived, loss_grads[0]], [copied]
    )[0]
    grad_own = landed_rows(grad_copies)
    own = after(own, arrived)
    other = other_core(own)
    forward_sent = after(forward_out, own)
    from_previous = shifted(forward_sent, 1)
    forward_partial = run_forward([own, other], weights, small, grad_copies)
    forward_received = other_core(forward_partial[1])
    own = after(grad_own, forward_partial[0])
    other = other_core(own)
    from_following = shifted(after(backward_out, own), -1)
    forward_pair = paired(forward_partial[0], forward_received, grad_copies)
    landed_forward = scattered(after(forward_pair, own))
    backward_partial = run_second_backward(own, other, projected, weights, small, forward_pair)
    backward_pair = paired(backward_partial[0], other_core(backward_partial[1]), from_following)
    landed_backward = scattered(backward_pair)
    from_previous = after(from_previous, backward_partial[0])
    forward_now = jnp.where(section == 0, fresh_streams[0], from_previous)
    evicted_second = to_partner(forward_now)
    backward_now = jnp.where(section == 15, loss_grads[0], from_following)
    forward_out = plain(
        forward_end_kernel, [scalars], [landed_forward, forward_now], [streams_out], backward_pair
    )[0]
    backward_out = plain(
        backward_end_kernel,
        [scalars],
        [landed_backward, backward_now, gain_row, *second_state],
        [streams_out],
        forward_out,
    )[0]
    evicted = jnp.stack([evicted_first, evicted_second])
    return (forward_out[None], backward_out[None], evicted[:, None])


def solution(mesh):
    return jax.shard_map(
        on_device,
        mesh=mesh,
        in_specs=(
            P("section", None, "tensor", None),
            P("section", None, "tensor", None),
            P(None, None, "tensor", None),
            P(None, None, "tensor", None),
            P(None, "section", None, "tensor", None),
            P(),
            P("section", None, "tensor"),
            P("section", None, None, "tensor"),
            P("section", "tensor", None),
            P("section", None),
            P("section", None, None),
            P("section", None),
            P("section", None),
            P("section", None, None),
        ),
        out_specs=(
            P("section", None, "tensor", None),
            P("section", None, "tensor", None),
            P(None, "section", None, "tensor", None),
        ),
        check_vma=False,
    )
```

```python
import functools
import math

import jax
import jax.numpy as jnp
import numpy as np
from jax import lax
from jax.experimental import pallas as pl
from jax.experimental.pallas import tpu as pltpu
from jax.sharding import PartitionSpec as P

EPSILON = 1e-06
ROPE_BASE = 1000000.0
ROWS = 128
LOCAL = 8
HEAD = 128
WIDTH = 5120
CHUNK = 2560
STEPS = WIDTH // CHUNK
QUERY = 384
BOTH = 256
GROUPS = [[core + 2 * chip for chip in range(8)] for core in range(2)]


def other_core(value):
    return lax.ppermute(value, "tensor", [(i, i ^ 1) for i in range(16)])


def to_partner(value):
    return lax.ppermute(value, "section", [(i, i ^ 8) for i in range(16)])


def shifted(value, by):
    return lax.ppermute(value, "section", [(i, (i + by) % 16) for i in range(16)])


def token_order(parity):
    own = [2 * chip + parity for chip in range(8)]
    other = [2 * chip + 1 - parity for chip in range(8)]
    return np.concatenate([np.arange(LOCAL) + LOCAL * block for block in own + other])


def tables_of(order):
    half = HEAD // 2
    frequency = np.float32(ROPE_BASE) ** (-np.arange(half, dtype=np.float32) / np.float32(half))
    angles = order.astype(np.float32)[:, None] * frequency[None, :]
    cosine, sine = np.cos(angles), np.sin(angles)
    mask = np.where(order[:, None] >= order[None, :], 0.0, -1e30)
    turn = order[:, None] == np.arange(ROWS)[None, :]
    planes = [np.concatenate([cosine, cosine], 1), np.concatenate([-sine, sine], 1), mask, turn]
    return np.stack(planes).astype(np.float32)


TABLES = np.stack([tables_of(token_order(0)), tables_of(token_order(1))])


def dot(left, right):
    return jnp.dot(left, right, preferred_element_type=jnp.float32)


def dot_nt(left, right):
    return lax.dot_general(left, right, (((1,), (1,)), ((), ())), preferred_element_type=jnp.float32)


def dot_tn(left, right):
    return lax.dot_general(left, right, (((0,), (0,)), ((), ())), preferred_element_type=jnp.float32)


def rope(values, cosine, sine):
    return values * cosine + pltpu.roll(values, HEAD // 2, 1) * sine


def rope_back(grads, cosine, sine):
    return grads * cosine - pltpu.roll(grads, HEAD // 2, 1) * sine


def norm_scale(values):
    return lax.rsqrt(jnp.mean(values * values, axis=-1, keepdims=True) + EPSILON)


def head_back(grads, values, scale, gain):
    weighted = grads * gain
    inner = jnp.mean(values * weighted, axis=-1, keepdims=True)
    return scale * weighted - values * (scale * scale * scale * inner)


def softmax_of(query_head, key_head, mask):
    scores = dot_nt(query_head, key_head) * (1.0 / math.sqrt(HEAD)) + mask
    scores = scores - jnp.max(scores, axis=-1, keepdims=True)
    weights = jnp.exp(scores)
    return weights / jnp.sum(weights, axis=-1, keepdims=True)


def joined(own, other, parity):
    first = jnp.where(parity == 0, own, other)
    second = jnp.where(parity == 0, other, own)
    return jnp.concatenate([first, second], axis=1)


def ordered(total, parity):
    own, other = total[:, QUERY : QUERY + HEAD], total[:, QUERY + HEAD :]
    half = HEAD // 2
    keys = joined(own[:, :half], other[:, :half], parity)
    values = joined(own[:, half:], other[:, half:], parity)
    return jnp.concatenate([total[:, :QUERY], keys, values], axis=1).astype(jnp.bfloat16)


def attend(projected, gains, cosine, sine, mask):
    bf16, f32 = jnp.bfloat16, jnp.float32
    keys = projected[:, QUERY : QUERY + HEAD].astype(f32)
    key_head = rope(keys * norm_scale(keys) * gains[1:2], cosine, sine).astype(bf16)
    values = projected[:, QUERY + HEAD :]
    context = []
    for head in range(QUERY // HEAD):
        queries = projected[:, head * HEAD : (head + 1) * HEAD].astype(f32)
        query_head = rope(queries * norm_scale(queries) * gains[0:1], cosine, sine).astype(bf16)
        weights = softmax_of(query_head, key_head, mask)
        context.append(dot(weights.astype(bf16), values).astype(bf16))
    return jnp.concatenate(context, axis=1)


def attend_back(projected, context_grad, gains, cosine, sine, mask, parity):
    bf16, f32 = jnp.bfloat16, jnp.float32
    root = 1.0 / math.sqrt(HEAD)
    keys = projected[:, QUERY : QUERY + HEAD].astype(f32)
    key_scale = norm_scale(keys)
    key_head = rope(keys * key_scale * gains[1:2], cosine, sine).astype(bf16)
    values = projected[:, QUERY + HEAD :]
    query_grads = []
    key_total = jnp.zeros((ROWS, HEAD), f32)
    value_total = jnp.zeros((ROWS, HEAD), f32)
    for head in range(QUERY // HEAD):
        queries = projected[:, head * HEAD : (head + 1) * HEAD].astype(f32)
        query_scale = norm_scale(queries)
        query_head = rope(queries * query_scale * gains[0:1], cosine, sine).astype(bf16)
        weights = softmax_of(query_head, key_head, mask)
        upstream = context_grad[:, head * HEAD : (head + 1) * HEAD].astype(bf16)
        value_total = value_total + dot_tn(weights.astype(bf16), upstream)
        weights_grad = dot_nt(upstream, values).astype(bf16).astype(f32)
        inner = jnp.sum(weights * weights_grad, axis=-1, keepdims=True)
        scores_grad = (weights * (weights_grad - inner) * root).astype(bf16)
        key_total = key_total + dot_tn(scores_grad, query_head)
        turned = rope_back(dot(scores_grad, key_head), cosine, sine)
        query_grads.append(head_back(turned, queries, query_scale, gains[0:1]).astype(bf16))
    key_grad = head_back(rope_back(key_total, cosine, sine), keys, key_scale, gains[1:2])
    half = HEAD // 2
    own = joined(key_grad[:, :half], value_total[:, :half], 0)
    other = joined(key_grad[:, half:], value_total[:, half:], 0)
    first = jnp.where(parity == 0, own, other)
    second = jnp.where(parity == 0, other, own)
    return jnp.concatenate(query_grads, axis=1), first.astype(bf16), second.astype(bf16)


PARAMS = pltpu.CompilerParams(vmem_limit_bytes=62 * 2**20)
SCALAR = pl.BlockSpec(memory_space=pltpu.SMEM)
FAR = pl.BlockSpec(memory_space=pl.ANY)
HALF = ROWS // 2
HALF_ROWS = jax.ShapeDtypeStruct((HALF, WIDTH), jnp.bfloat16)
BF = jnp.bfloat16


def started(copies):
    for copy in copies:
        copy.start()
    return copies


def waited(copies):
    for copy in copies:
        copy.wait()


def columns(chunk):
    return pl.ds(chunk * CHUNK, CHUNK)


def query_loads(queries_w, own_w, other_w, near, sems):
    near_q, near_own, near_other = near
    return [
        [
            pltpu.make_async_copy(
                queries_w.at[columns(c), :], near_q.at[columns(c), :], sems.at[c, 0]
            ),
            pltpu.make_async_copy(own_w.at[:, columns(c)], near_own.at[:, columns(c)], sems.at[c, 1]),
            pltpu.make_async_copy(
                other_w.at[:, columns(c)], near_other.at[:, columns(c)], sems.at[c, 2]
            ),
        ]
        for c in range(STEPS)
    ]


def output_loads(output_w, near, sems):
    return [
        [pltpu.make_async_copy(output_w.at[:, columns(c)], near.at[:, columns(c)], sems.at[c])]
        for c in range(STEPS)
    ]


def row_loads(own, other, rows, sems, part=0):
    if other is None:
        return [pltpu.make_async_copy(own, rows, sems.at[0])]
    source = pl.ds(part * WIDTH, WIDTH)
    return [
        pltpu.make_async_copy(own.at[:, source], rows.at[pl.ds(0, HALF), :], sems.at[0]),
        pltpu.make_async_copy(other.at[:, source], rows.at[pl.ds(HALF, HALF), :], sems.at[1]),
    ]


def stores(near, mine, theirs, c, sems):
    return [
        pltpu.make_async_copy(
            near.at[pl.ds(HALF, HALF), columns(c)], theirs.at[:, columns(c)], sems.at[c, 0]
        ),
        pltpu.make_async_copy(
            near.at[pl.ds(0, HALF), columns(c)], mine.at[:, columns(c)], sems.at[c, 1]
        ),
    ]


def project_chunks(rows, near, loads):
    near_q, near_own, near_other = near
    queries = own = other = 0.0
    for c in range(STEPS):
        waited(loads[c])
        part = rows[:, c * CHUNK : (c + 1) * CHUNK]
        queries += dot(part, near_q[c * CHUNK : (c + 1) * CHUNK, :])
        own += dot_nt(part, near_own[:, c * CHUNK : (c + 1) * CHUNK])
        other += dot_nt(part, near_other[:, c * CHUNK : (c + 1) * CHUNK])
    return jnp.concatenate([queries, own, other], axis=1)


WEIGHT_SCRATCH = [
    pltpu.VMEM((WIDTH, QUERY), BF),
    pltpu.VMEM((HEAD, WIDTH), BF),
    pltpu.VMEM((HEAD, WIDTH), BF),
    pltpu.SemaphoreType.DMA((STEPS, 3)),
]
ROW_SCRATCH = [pltpu.VMEM((ROWS, WIDTH), BF), pltpu.SemaphoreType.DMA((2,))]
SMALL_SCRATCH = [
    pltpu.VMEM((2, HEAD), jnp.float32),
    pltpu.VMEM((4, ROWS, HEAD), jnp.float32),
    pltpu.SemaphoreType.DMA((2,)),
]
OUT_SCRATCH = [pltpu.VMEM((ROWS, WIDTH), BF), pltpu.SemaphoreType.DMA((STEPS, 2))]


def small_loads(gains, tables, near_gains, near_tables, sems):
    return [
        pltpu.make_async_copy(gains, near_gains, sems.at[0]),
        pltpu.make_async_copy(tables, near_tables, sems.at[1]),
    ]


def forward_kernel(
    turned, parity, *refs
):
    own, other = refs[0], None if turned else refs[1]
    queries_w, own_w, other_w, output_w, gains, tables, _, *rest = refs[1 if turned else 2 :]
    mine, theirs, near_q, near_own, near_other, weight_sems, rows, row_sems = rest[:8]
    near_gains, near_tables, small_sems, near_out, out_sems, near_output_w, output_sems = rest[8:15]
    near = (near_q, near_own, near_other)
    row_copies = started(row_loads(own, other, rows, row_sems))
    loads = [started(part) for part in query_loads(queries_w, own_w, other_w, near, weight_sems)]
    small_copies = started(small_loads(gains, tables, near_gains, near_tables, small_sems))
    output_copies = [started(part) for part in output_loads(output_w, near_output_w, output_sems)]
    waited(row_copies)
    projected = ordered(project_chunks(rows, near, loads), parity[0])
    waited(small_copies)
    if turned:
        projected = dot(near_tables[3].astype(BF), projected).astype(BF)
    context = attend(projected, near_gains[...], near_tables[0], near_tables[1], near_tables[2])
    sent = []
    for c in range(STEPS):
        waited(output_copies[c])
        part = dot(context, near_output_w[:, c * CHUNK : (c + 1) * CHUNK])
        near_out[:, c * CHUNK : (c + 1) * CHUNK] = part.astype(BF)
        sent += started(stores(near_out, mine, theirs, c, out_sems))
    waited(sent)


def project_kernel(
    parity, own, other, queries_w, own_w, other_w, after, out,
    near_q, near_own, near_other, weight_sems, rows, row_sems, near_out, sems,
):
    del after
    near = (near_q, near_own, near_other)
    row_copies = started(row_loads(own, other, rows, row_sems, 2))
    loads = [started(part) for part in query_loads(queries_w, own_w, other_w, near, weight_sems)]
    waited(row_copies)
    projected = ordered(project_chunks(rows, near, loads), parity[0])
    near_out[...] = projected
    waited(started([pltpu.make_async_copy(near_out, out, sems.at[0])]))


def context_kernel(
    part, own, other, output_w, after, out, rows, row_sems, near_output_w, output_sems, near_out, sems
):
    del after
    row_copies = started(row_loads(own, other, rows, row_sems, part))
    output_copies = [started(chunk) for chunk in output_loads(output_w, near_output_w, output_sems)]
    waited(row_copies)
    near_out[...] = context_chunks(rows, near_output_w, output_copies)
    waited(started([pltpu.make_async_copy(near_out, out, sems.at[0])]))


def context_chunks(rows, near_output_w, output_copies):
    context_grad = 0.0
    for c in range(STEPS):
        waited(output_copies[c])
        part = slice(c * CHUNK, (c + 1) * CHUNK)
        context_grad += dot_nt(rows[:, part], near_output_w[:, part])
    return context_grad


def grads_out(grads, near, loads, near_out, mine, theirs, out_sems):
    query_grad, own_grad, other_grad = grads
    near_q, near_own, near_other = near
    sent = []
    for c in range(STEPS):
        waited(loads[c])
        part = slice(c * CHUNK, (c + 1) * CHUNK)
        total = dot_nt(query_grad, near_q[part, :])
        total = total + dot(own_grad, near_own[:, part]) + dot(other_grad, near_other[:, part])
        near_out[:, part] = total.astype(BF)
        sent += started(stores(near_out, mine, theirs, c, out_sems))
    waited(sent)


def first_backward_kernel(
    parity, own, other, context_grad, queries_w, own_w, other_w, gains, tables, after, mine, theirs,
    near_q, near_own, near_other, weight_sems, rows, row_sems, near_gains, near_tables, small_sems,
    near_out, out_sems, near_context, context_sem,
):
    del after
    near = (near_q, near_own, near_other)
    row_copies = started(row_loads(own, other, rows, row_sems))
    loads = [started(part) for part in query_loads(queries_w, own_w, other_w, near, weight_sems)]
    small_copies = started(small_loads(gains, tables, near_gains, near_tables, small_sems))
    small_copies += started([pltpu.make_async_copy(context_grad, near_context, context_sem.at[0])])
    waited(row_copies)
    projected = ordered(project_chunks(rows, near, loads), parity[0])
    waited(small_copies)
    grads = attend_back(
        projected, near_context[...], near_gains[...], near_tables[0], near_tables[1], near_tables[2], parity[0]
    )
    grads_out(grads, near, [[]] * STEPS, near_out, mine, theirs, out_sems)


def second_backward_kernel(
    parity, own, other, projected, queries_w, own_w, other_w, output_w, gains, tables, after, mine, theirs,
    near_q, near_own, near_other, weight_sems, rows, row_sems, near_gains, near_tables, small_sems,
    near_out, out_sems, near_output_w, output_sems, near_projected, projected_sem,
):
    del after
    near = (near_q, near_own, near_other)
    row_copies = started(row_loads(own, other, rows, row_sems))
    output_copies = [started(part) for part in output_loads(output_w, near_output_w, output_sems)]
    small_copies = started(small_loads(gains, tables, near_gains, near_tables, small_sems))
    small_copies += started([pltpu.make_async_copy(projected, near_projected, projected_sem.at[0])])
    loads = [started(part) for part in query_loads(queries_w, own_w, other_w, near, weight_sems)]
    waited(row_copies)
    context_grad = context_chunks(rows, near_output_w, output_copies)
    waited(small_copies)
    grads = attend_back(
        near_projected[...], context_grad, near_gains[...], near_tables[0], near_tables[1], near_tables[2], parity[0]
    )
    grads_out(grads, near, loads, near_out, mine, theirs, out_sems)


def far_call(kernel, scalars, arrays, out_shape, scratch, time):
    return pl.pallas_call(
        kernel,
        out_shape=out_shape,
        in_specs=[SCALAR] * len(scalars) + [FAR] * len(arrays),
        out_specs=[FAR] * len(out_shape),
        scratch_shapes=scratch,
        compiler_params=PARAMS,
        cost_estimate=pl.CostEstimate(
            flops=time * 1000000000, bytes_accessed=1000, transcendentals=0
        ),
    )(*scalars, *arrays)


OUTPUT_SCRATCH = [pltpu.VMEM((QUERY, WIDTH), BF), pltpu.SemaphoreType.DMA((STEPS,))]
MAIN_SCRATCH = WEIGHT_SCRATCH + ROW_SCRATCH + SMALL_SCRATCH + OUT_SCRATCH
PROJECTED = jax.ShapeDtypeStruct((ROWS, QUERY + BOTH), BF)
CONTEXT = jax.ShapeDtypeStruct((ROWS, QUERY), jnp.float32)


def run_forward(gathered_rows, weights, small, after):
    arrays = [*gathered_rows, *weights, *small[1:], after]
    scratch = MAIN_SCRATCH + OUTPUT_SCRATCH
    kernel = functools.partial(forward_kernel, len(gathered_rows) == 1)
    return far_call(kernel, small[:1], arrays, [HALF_ROWS] * 2, scratch, 8)


def run_project(own, other, weights, small, after):
    scratch = [pltpu.VMEM(PROJECTED.shape, BF), pltpu.SemaphoreType.DMA((1,))]
    arrays = [own, other, *weights[:3], after]
    scratch = WEIGHT_SCRATCH + ROW_SCRATCH + scratch
    return far_call(project_kernel, small[:1], arrays, [PROJECTED], scratch, 5)[0]


def run_context(own, other, part, output_w, after):
    scratch = [pltpu.VMEM(CONTEXT.shape, CONTEXT.dtype), pltpu.SemaphoreType.DMA((1,))]
    kernel = functools.partial(context_kernel, part)
    arrays = [own, other, output_w, after]
    return far_call(kernel, [], arrays, [CONTEXT], ROW_SCRATCH + OUTPUT_SCRATCH + scratch, 4)[0]


def run_first_backward(own, other, context_grad, weights, small, after):
    scratch = [pltpu.VMEM(CONTEXT.shape, CONTEXT.dtype), pltpu.SemaphoreType.DMA((1,))]
    arrays = [own, other, context_grad, *weights[:3], *small[1:], after]
    outs = [HALF_ROWS] * 2
    return far_call(first_backward_kernel, small[:1], arrays, outs, MAIN_SCRATCH + scratch, 12)


def run_second_backward(own, other, projected, weights, small, after):
    scratch = [pltpu.VMEM(PROJECTED.shape, BF), pltpu.SemaphoreType.DMA((1,))]
    arrays = [own, other, projected, *weights, *small[1:], after]
    scratch = MAIN_SCRATCH + OUTPUT_SCRATCH + scratch
    return far_call(second_backward_kernel, small[:1], arrays, [HALF_ROWS] * 2, scratch, 12)


def mixed(weights, offset, stride, streams):
    return sum(weights[offset + i * stride] * streams[i] for i in range(4))


def normed_rows(scalars, streams, gain):
    total = mixed(scalars, 0, 1, streams.astype(jnp.float32))
    scale = norm_scale(total)
    return (total * scale * gain).astype(BF), total, scale


def out_grad_rows(scalars, grads):
    return mixed(scalars, 4, 1, grads.astype(jnp.float32)).astype(BF)


def front_kernel(scalars, slot, saved, grads, gain, every, *states):
    for tick in range(2):
        combined, scale = states[2 * tick : 2 * tick + 2]
        chosen = slot[0] if tick == 0 else 1 - slot[0]
        normed, combined[...], row_scale = normed_rows(scalars, saved[chosen], gain[...])
        every[:, 2 * tick * WIDTH : (2 * tick + 1) * WIDTH] = normed
        scale[...] = jnp.broadcast_to(row_scale, scale.shape)
    every[:, WIDTH : 2 * WIDTH] = out_grad_rows(scalars, grads[...])


def norm_kernel(scalars, streams, gain, normed):
    normed[...] = normed_rows(scalars, streams[...], gain[...])[0]


def next_norm_kernel(scalars, local, arrived, fresh, gain, normed):
    rows = normed_rows(scalars, fresh[...], gain[...])[0]
    normed[...] = jnp.where(local[0] == 1, rows, arrived[...])


def next_grad_kernel(scalars, local, arrived, loss, out_grad):
    out_grad[...] = jnp.where(local[0] == 1, out_grad_rows(scalars, loss[...]), arrived[...])


def pair_kernel(mine, received, out):
    pair = mine[...].astype(jnp.float32) + received[...].astype(jnp.float32)
    out[...] = pair.astype(out.dtype)


def forward_end_kernel(scalars, landed, streams, out):
    rows = jnp.sum(landed[...].astype(jnp.float32), axis=0)
    streams_f = streams[...].astype(jnp.float32)
    for i in range(4):
        out[i] = (mixed(scalars, 8 + 4 * i, 1, streams_f) + scalars[4 + i] * rows).astype(out.dtype)


def forward_next_kernel(scalars, following, landed, streams, next_gain, out, normed):
    forward_end_kernel(scalars, landed, streams, out)
    normed[...] = normed_rows(following, out[...], next_gain[...])[0]


def backward_next_kernel(scalars, preceding, landed, grads, gain, combined, scale, out, out_grad):
    backward_end_kernel(scalars, landed, grads, gain, combined, scale, out)
    out_grad[...] = out_grad_rows(preceding, out[...])


def backward_end_kernel(scalars, landed, grads, gain, combined, scale, out):
    weighted = jnp.sum(landed[...].astype(jnp.float32), axis=0) * gain[...]
    row_scale = scale[:, :1]
    inner = jnp.mean(weighted * combined[...], axis=-1, keepdims=True)
    combined_grad = row_scale * weighted - combined[...] * (row_scale * row_scale * row_scale * inner)
    grads_f = grads[...].astype(jnp.float32)
    for j in range(4):
        out[j] = (mixed(scalars, 8 + j, 4, grads_f) + scalars[j] * combined_grad).astype(out.dtype)


def plain(kernel, scalars, arrays, outs, after=None):
    n, m, k = len(scalars), len(arrays), len(outs)
    extra = [] if after is None else [after]
    e = len(extra)

    def body(*refs):
        far_in, far_out = refs[n : n + m], refs[n + m + e : n + m + e + k]
        rest = refs[n + m + e + k :]
        near_in, near_out, sems, out_sems = rest[:m], rest[m : m + k], rest[m + k], rest[m + k + 1]
        waited(
            started([pltpu.make_async_copy(far_in[i], near_in[i], sems.at[i]) for i in range(m)])
        )
        kernel(*refs[:n], *near_in, *near_out)
        sent = []
        for i in range(k):
            if outs[i][2]:
                for chip in range(8):
                    sent.append(
                        pltpu.make_async_copy(near_out[i], far_out[i].at[chip], out_sems.at[i, chip])
                    )
            else:
                sent.append(pltpu.make_async_copy(near_out[i], far_out[i], out_sems.at[i, 0]))
        waited(started(sent))

    shapes = [((8,) if out[2] else ()) + out[0] for out in outs]
    return pl.pallas_call(
        body,
        out_shape=[jax.ShapeDtypeStruct(shape, out[1]) for shape, out in zip(shapes, outs)],
        in_specs=[SCALAR] * n + [FAR] * (m + e),
        out_specs=[FAR] * k,
        scratch_shapes=[pltpu.VMEM(array.shape, array.dtype) for array in arrays]
        + [pltpu.VMEM(out[0], out[1]) for out in outs]
        + [pltpu.SemaphoreType.DMA((m,)), pltpu.SemaphoreType.DMA((k, 8))],
        compiler_params=PARAMS,
        cost_estimate=pl.CostEstimate(flops=2500000000, bytes_accessed=1000, transcendentals=0),
    )(*scalars, *arrays, *extra)


def after(value, *events):
    return lax.optimization_barrier((value, *events))[0]


def landed_rows(copies):
    own = lax.all_to_all(copies, "tensor", 0, 0, axis_index_groups=GROUPS, tiled=True)
    return own.reshape(HALF, -1)


def paired(mine, received, event):
    pair = after(mine, event).astype(jnp.float32) + received.astype(jnp.float32)
    return pair.astype(jnp.bfloat16)


def scattered(pair):
    return lax.all_to_all(
        pair.reshape(8, LOCAL, -1), "tensor", 0, 0, axis_index_groups=GROUPS, tiled=True
    )


def on_device(
    entering_streams,
    entering_grads,
    fresh_streams,
    loss_grads,
    stashed,
    slot_order,
    q_weight,
    kv_weight,
    out_weight,
    norm_gain,
    head_gains,
    stream_in,
    stream_out,
    stream_mix,
):
    section = lax.axis_index("section")
    parity = lax.axis_index("tensor") % 2
    partner = (section + 8) % 16
    queries_w, output_w = q_weight[0], out_weight[0]
    gain, gains = norm_gain[0], head_gains[0]
    mix_in, mix_out, mix = stream_in[0], stream_out[0], stream_mix[0]
    bf16, f32 = jnp.bfloat16, jnp.float32

    tables = jnp.where(parity == 0, jnp.asarray(TABLES[0]), jnp.asarray(TABLES[1]))

    own_w = jnp.swapaxes(kv_weight[0], 1, 2).reshape(HEAD, -1)
    other_w = other_core(own_w)
    weights = (queries_w, own_w, other_w, output_w)
    small = (parity[None].astype(jnp.int32), gains, tables)
    gain_row, mix_flat = gain[None], mix.reshape(16)
    row_shape, streams_shape = (LOCAL, WIDTH), (4, LOCAL, WIDTH)
    row, copied = (row_shape, bf16, False), (row_shape, bf16, True)
    streams_out = (streams_shape, bf16, False)
    state_outs = [(row_shape, f32, False), ((LOCAL, HEAD), f32, False)]

    scalars = jnp.concatenate([mix_in, mix_out, mix_flat])
    saved = to_partner(stashed[:, 0])
    forward_now, backward_now = entering_streams[0], entering_grads[0]
    params = jnp.concatenate([gain, scalars, jnp.zeros((104,), f32)])[None]
    params = shifted(params, -1)
    preceding = shifted(scalars, 1)
    at_start = (section == 0).astype(jnp.int32)[None]
    at_end = (section == 15).astype(jnp.int32)[None]
    slot = slot_order[section, 0][None]
    normed = plain(norm_kernel, [scalars], [forward_now, gain_row], [copied])[0]
    normed, saved, params, preceding = lax.optimization_barrier((normed, saved, params, preceding))
    next_gain, following = params[:, :WIDTH], params[0, WIDTH : WIDTH + 24]
    own = landed_rows(normed)
    other = other_core(own)

    both_out = ((LOCAL, 3 * WIDTH), bf16, True)
    both, *states = plain(
        front_kernel, [scalars, slot], [saved, backward_now, gain_row], [both_out] + state_outs * 2, normed
    )
    first_state, second_state = states[:2], states[2:]
    both_own = landed_rows(both)

    forward_partial = run_forward([own, other], weights, small, both)
    forward_received = other_core(forward_partial[1])
    forward_pair = paired(forward_partial[0], forward_received, forward_partial[0])
    evicted_first = to_partner(forward_now)
    both_own = after(both_own, forward_pair, evicted_first)
    both_other = other_core(both_own)
    landed = scattered(forward_pair)

    context_grad = run_context(both_own, both_other, 1, output_w, evicted_first)
    backward_partial = run_first_backward(both_own, both_other, context_grad, weights, small, context_grad)
    backward_received = other_core(backward_partial[1])
    forward_out, next_normed = plain(
        forward_next_kernel,
        [scalars, following],
        [landed, forward_now, next_gain],
        [streams_out, row],
        backward_partial[0],
    )
    arrived = shifted(next_normed, 1)

    backward_pair = paired(backward_partial[0], backward_received, forward_out)
    landed = scattered(after(backward_pair, arrived))
    arrived = after(arrived, backward_pair)
    normed_copies = plain(
        next_norm_kernel, [scalars, at_start], [arrived, fresh_streams[0], gain_row], [copied]
    )[0]
    projected = run_project(both_own, both_other, weights, small, normed_copies)
    own = landed_rows(after(normed_copies, projected))
    backward_out, next_grad = plain(
        backward_next_kernel,
        [scalars, preceding],
        [landed, backward_now, gain_row, *first_state],
        [streams_out, row],
        projected,
    )
    arrived = shifted(next_grad, -1)

    grad_copies = plain(
        next_grad_kernel, [scalars, at_end], [arrived, loss_grads[0]], [copied]
    )[0]
    grad_own = landed_rows(grad_copies)
    own = after(own, arrived)
    other = other_core(own)
    forward_sent = after(forward_out, own)
    from_previous = shifted(forward_sent, 1)
    forward_partial = run_forward([own, other], weights, small, grad_copies)
    forward_received = other_core(forward_partial[1])
    own = after(grad_own, forward_partial[0])
    other = other_core(own)
    from_following = shifted(after(backward_out, own), -1)
    forward_pair = paired(forward_partial[0], forward_received, grad_copies)
    landed_forward = scattered(after(forward_pair, own))
    backward_partial = run_second_backward(own, other, projected, weights, small, forward_pair)
    backward_pair = paired(backward_partial[0], other_core(backward_partial[1]), from_following)
    landed_backward = scattered(backward_pair)
    from_previous = after(from_previous, backward_partial[0])
    forward_now = jnp.where(section == 0, fresh_streams[0], from_previous)
    evicted_second = to_partner(forward_now)
    backward_now = jnp.where(section == 15, loss_grads[0], from_following)
    forward_out = plain(
        forward_end_kernel, [scalars], [landed_forward, forward_now], [streams_out], backward_pair
    )[0]
    backward_out = plain(
        backward_end_kernel,
        [scalars],
        [landed_backward, backward_now, gain_row, *second_state],
        [streams_out],
        forward_out,
    )[0]
    evicted = jnp.stack([evicted_first, evicted_second])
    return (forward_out[None], backward_out[None], evicted[:, None])


def solution(mesh):
    return jax.shard_map(
        on_device,
        mesh=mesh,
        in_specs=(
            P("section", None, "tensor", None),
            P("section", None, "tensor", None),
            P(None, None, "tensor", None),
            P(None, None, "tensor", None),
            P(None, "section", None, "tensor", None),
            P(),
            P("section", None, "tensor"),
            P("section", None, None, "tensor"),
            P("section", "tensor", None),
            P("section", None),
            P("section", None, None),
            P("section", None),
            P("section", None),
            P("section", None, None),
        ),
        out_specs=(
            P("section", None, "tensor", None),
            P("section", None, "tensor", None),
            P(None, "section", None, "tensor", None),
        ),
        check_vma=False,
    )
```
